256 devices in a mesh: ia: 8 (over x, core), ja: 32 (over y, z).
Axes of the slice: x: 4, y: 4, z: 8, core: 2. Of those that a mesh axis runs over, the one named last changes fastest.
Arguments:
- state: float32 [12, 65536], P(None, 'ja'), may hold values from -6 to 6
- mass: float32 [65536], P('ja'), may hold values from 0.2 to 5
- elapsed: float32 [65536], P('ja'), may hold values from 0.05 to 0.5
- active_ids: int32 [16384], P('ia'), may hold values from 0 to 65535, as said below
- active_count: int32 [8], replicated, may hold values from 256 to 2048, as said below
Outputs:
- new_state: float32 [12, 65536], P(None, 'ja')
- active_force: float32 [6, 16384], P(None, 'ia')
The draws below stay inside these ranges and needn't reach their ends.
Inputs may be any that keep to these rules, and one draw needn't show every extreme that they name: `active_ids`: all entries are distinct star numbers. `active_count`: one list in every draw is full.
All inputs are finite; a program needn't handle non-finite values.
Results may differ from the reference program's by a relative error of at most 0.000047.
Values sent between devices are 32-bit elements; how exact they have to be, the bound alone decides.
No kernel may reach another device: no remote copies, remote signals or barrier semaphores. Data moves between devices by JAX's collectives and lax.ppermute only.
A program may use at most 64 MiB of HBM per device.

```python
import math
import jax
import jax.numpy as jnp
from jax import lax

ACT_CAP = 2048
STARS = 65536
N_IA = 8


def draw_active_ids(key, part):
    key = jax.random.fold_in(key, 11)
    order = jax.random.permutation(key, STARS)
    chosen = order[:N_IA * ACT_CAP].astype(jnp.int32)
    position = jnp.arange(N_IA * ACT_CAP, dtype=jnp.int32)
    has_top = jnp.any(chosen == STARS - 1)
    chosen = jnp.where((position == 0) & ~has_top, STARS - 1, chosen)
    has_zero = jnp.any(chosen == 0)
    chosen = jnp.where((position == 1) & ~has_zero, 0, chosen)
    return chosen.astype(jnp.int32)


def draw_active_count(key, part):
    key = jax.random.fold_in(key, 23)
    first, second, third = jax.random.split(key, 3)
    counts = jax.random.randint(first, (N_IA,), ACT_CAP // 8, ACT_CAP // 2 + 1)
    busiest = jax.random.randint(second, (), 0, N_IA)
    lightest = (busiest + 1 + jax.random.randint(third, (), 0, N_IA - 1)) % N_IA
    counts = jnp.where(jnp.arange(N_IA) == busiest, ACT_CAP, counts)
    counts = jnp.where(jnp.arange(N_IA) == lightest, ACT_CAP // 8, counts)
    return counts.astype(jnp.int32)


def block_levels(key, extent, pieces, low, high):
    factor_of = 1.0
    for dim, shards_of in pieces:
        heights = jax.random.uniform(jax.random.fold_in(jax.random.fold_in(key, 6), dim), (shards_of,), jnp.float32, low / len(pieces), high / len(pieces))
        factor_of = factor_of * jnp.repeat(jnp.exp(heights), extent[dim] // shards_of).reshape((-1,) + (1,) * (len(extent) - 1 - dim))
    return factor_of


def noise(stream_key, dims, width, bound, cuts=(), kind=jnp.bfloat16):
    gain = block_levels(stream_key, dims, cuts, -0.22, 0.18) if cuts else 1.0
    result = jax.random.normal(stream_key, dims, jnp.float32) * width * gain
    return jnp.minimum(jnp.maximum(result, -bound), bound).astype(kind)


def setup_inputs(seed: int = 0) -> dict:
    keys = jax.random.split(jax.random.key(seed), 6)
    state = noise(keys[0], (12, STARS), 1.0, 6.0, ((1, 32),), jnp.float32)
    mass = jnp.clip(jnp.exp(math.log(5.0) - 3.218876 * jax.random.uniform(keys[1], (STARS,), jnp.float32) ** block_levels(keys[1], (STARS,), ((0, 32),), -0.2, 0.2)), 0.2, 5.0)
    elapsed = jnp.clip(jnp.exp(math.log(0.5) - 2.3025851 * jax.random.uniform(keys[2], (STARS,), jnp.float32) ** block_levels(keys[2], (STARS,), ((0, 32),), -0.2, 0.2)), 0.05, 0.5)
    active_ids = draw_active_ids(jax.random.fold_in(keys[5], 71), 0)
    active_count = draw_active_count(jax.random.fold_in(keys[5], 71), 0)
    return {"state": state, "mass": mass, "elapsed": elapsed, "active_ids": active_ids, "active_count": active_count}


softening_square = 0.01

def predict(state, elapsed):
    position = state[0:3]
    velocity = state[3:6]
    accel_old = state[6:9]
    jerk_old = state[9:12]
    half = elapsed * elapsed * 0.5
    sixth = half * elapsed / 3.0
    new_pos = position + velocity * elapsed + accel_old * half + jerk_old * sixth
    new_vel = velocity + accel_old * elapsed + jerk_old * half
    return (new_pos, new_vel)

def pair_terms(target_pos, target_vel, source_pos, source_vel, source_mass, scale):
    separation = source_pos[:, None, :] - target_pos[:, :, None]
    relative = source_vel[:, None, :] - target_vel[:, :, None]
    square = lax.optimization_barrier(jnp.sum(separation * separation, axis=0)) + softening_square
    inverse = 1.0 / jnp.sqrt(square)
    weight = source_mass[None, :] * inverse * inverse * inverse * scale
    radial = 3.0 * lax.optimization_barrier(jnp.sum(separation * relative, axis=0)) / square
    accel_sum = lax.optimization_barrier(jnp.sum(weight[None] * separation, axis=2))
    jerk_sum = lax.optimization_barrier(jnp.sum(weight[None] * (relative - radial[None] * separation), axis=2))
    return jnp.concatenate([accel_sum, jerk_sum], axis=0)

def correct(old, step_time, force):
    position = old[0:3]
    velocity = old[3:6]
    accel_old = old[6:9]
    jerk_old = old[9:12]
    accel_new = force[0:3]
    jerk_new = force[3:6]
    half = step_time * 0.5
    twelfth = step_time * step_time / 12.0
    vel_new = velocity + (accel_old + accel_new) * half + (jerk_old - jerk_new) * twelfth
    pos_new = position + (velocity + vel_new) * half + (accel_old - accel_new) * twelfth
    return jnp.concatenate([pos_new, vel_new, accel_new, jerk_new], axis=0)

def reference(state, mass, elapsed, active_ids, active_count):
    scale = 1.0 / STARS
    pred_pos, pred_vel = predict(state, elapsed)
    slots = jnp.arange(ACT_CAP * N_IA)
    valid = slots % ACT_CAP < active_count[slots // ACT_CAP]
    groups = active_ids.reshape(-1, 128)

    def one_group(group):
        return pair_terms(pred_pos[:, group], pred_vel[:, group], pred_pos, pred_vel, mass, scale)
    force = lax.map(one_group, groups)
    force = jnp.transpose(force, (1, 0, 2)).reshape(6, -1)
    old = state[:, active_ids]
    step_time = elapsed[active_ids]
    fresh = correct(old, step_time, force)
    target = jnp.where(valid, active_ids, STARS).astype(jnp.int32)
    new_state = state.at[:, target].set(fresh, mode='drop')
    active_force = jnp.where(valid[None], force, jnp.float32(0.0))
    return (new_state, active_force)
```

```python
import jax
import jax.numpy as jnp
from jax import lax
from jax.experimental import pallas as pl
from jax.experimental.pallas import tpu as pltpu
from jax.sharding import Mesh, PartitionSpec as P

F32 = jnp.float32
I32 = jnp.int32
softening_square = 0.01
LISTS = 8
CAP = 2048
SHARD = 2048
GROUPS = 64
LANES = 128
BLOCKS = 128
SMEM = pl.BlockSpec(memory_space=pltpu.SMEM)
VMEM = pl.BlockSpec(memory_space=pltpu.VMEM)


def take(tile, index):
    return jnp.take_along_axis(tile, index, axis=1, mode="promise_in_bounds")


def list_offsets(counts_ref):
    offsets = [jnp.int32(0)]
    for i in range(LISTS):
        offsets.append(offsets[-1] + counts_ref[i])
    return offsets[:LISTS], offsets[LISTS]


def group_size(live):
    return lax.shift_right_logical(live + (GROUPS - 1), 6)


def split_position(position, size):
    group = jnp.floor((position.astype(F32) + 0.5) / size.astype(F32)).astype(I32)
    lane = position - group * size
    return group * 2 + (lane >> 7), lane & 127


def pack_kernel(state_ref, mass_ref, elapsed_ref, ids_ref, out_ref):
    eighth = lax.axis_index("x") * 2 + lax.axis_index("c")
    part = pl.ds(pl.multiple_of(eighth * 256, 256), 256)
    piece = pl.ds(pl.multiple_of(lax.axis_index("z") * 256, 256), 256)
    old = state_ref[:, part]
    step = elapsed_ref[:, part]
    half = step * step * 0.5
    sixth = half * step / 3.0
    pos = old[0:3] + old[3:6] * step + old[6:9] * half + old[9:12] * sixth
    vel = old[3:6] + old[6:9] * step + old[9:12] * half
    mass = mass_ref[:, part] * (1.0 / 65536.0)
    ids = ids_ref[:, piece].astype(F32)
    rows = jnp.concatenate([pos, vel, mass, ids], axis=0)
    both = jnp.concatenate([rows[:, :LANES], rows[:, LANES:]], axis=0)
    for peer in range(32):
        out_ref[peer] = both


def extract_kernel(counts_ref, slab_ref, out_ref):
    offsets, live = list_offsets(counts_ref)
    size = group_size(live)
    group = lax.axis_index("c") * 32 + lax.axis_index("x") * 8 + lax.axis_index("z")
    my_y = lax.axis_index("y")
    sub = lax.broadcasted_iota(I32, (8, LANES), 0)
    column = lax.broadcasted_iota(I32, (8, LANES), 1)

    def one_half(half):
        lane = column + half * LANES
        position = group * size + lane
        valid = (lane < size) & (position < live)
        which = jnp.zeros((8, LANES), I32)
        base = jnp.zeros((8, LANES), I32)
        for i in range(1, LISTS):
            after = position >= offsets[i]
            which = jnp.where(after, i, which)
            base = jnp.where(after, offsets[i], base)
        slot = jnp.where(valid, position - base, 0)
        block = (which & 1) * 64 + (which >> 1) * 16 + (slot >> 8) * 2 + ((slot >> 7) & 1)
        within = slot & 127
        found = jnp.zeros((8, LANES), F32)
        for v in range(16):
            tile = slab_ref[pl.ds(7 + 64 * v, 8, stride=8), :]
            found = jnp.where(block == v * 8 + sub, take(tile, within), found)
        star = jnp.broadcast_to(jnp.sum(found, axis=0, keepdims=True), (8, LANES)).astype(I32)
        mine = valid & ((star >> 14) == my_y)
        place = ((star >> 8) & 1) * 64 + ((star >> 9) & 3) * 16 + ((star >> 11) & 7) * 2 + ((star >> 7) & 1)
        place = jnp.where(mine, place, -1)
        inside = star & 127

        def step(turn, acc):
            for k in range(16):
                b = turn * 16 + k
                tile = slab_ref[pl.ds(pl.multiple_of(b * 8, 8), 8), :]
                acc = jnp.where(place == b, take(tile, inside), acc)
            return acc

        picked = lax.fori_loop(0, BLOCKS // 16, step, jnp.zeros((8, LANES), F32))
        out_ref[half * 8 : half * 8 + 8, :] = jnp.where(sub < 6, picked, 0.0)

    one_half(0)
    out_ref[8:16, :] = jnp.zeros((8, LANES), F32)

    @pl.when(size > LANES)
    def _():
        one_half(1)


def inverse_kernel(counts_ref, slab_ref, block_ref, lane_ref):
    offsets, live = list_offsets(counts_ref)
    size = group_size(live)
    shard = lax.axis_index("y") * 8 + lax.axis_index("z")
    wide = 2 * LANES
    row16 = lax.broadcasted_iota(I32, (16, wide), 0)
    row128 = lax.broadcasted_iota(I32, (LANES, wide), 0)
    column = lax.broadcasted_iota(I32, (1, wide), 1)
    total = jnp.zeros((32, LANES), F32)
    for i in range(LISTS):
        first = ((i & 1) * 32 + (i >> 1) * 8) * 16

        def step(turn, acc):
            row = first + turn * 16
            ids = jnp.concatenate(
                [slab_ref[pl.ds(row + 7, 1), :], slab_ref[pl.ds(row + 15, 1), :]], axis=1
            ).astype(I32)
            slot = turn * wide + column
            mine = (slot < counts_ref[i]) & ((ids >> 11) == shard)
            high = jnp.where(mine, (ids >> 7) & 15, -1)
            low = ids & 127
            mark = offsets[i] + slot + 1
            here = row16 == high
            left = jnp.concatenate(
                [
                    jnp.where(here, (mark >> 7).astype(F32), 0.0),
                    jnp.where(here, (mark & 127).astype(F32), 0.0),
                ],
                axis=0,
            ).astype(jnp.bfloat16)
            right = jnp.where(row128 == low, 1.0, 0.0).astype(jnp.bfloat16)
            return acc + lax.dot_general(
                left, right, (((1,), (1,)), ((), ())), preferred_element_type=F32
            )

        total = lax.fori_loop(0, (counts_ref[i] + (wide - 1)) >> 8, step, total)
    position = (total[0:16] * 128.0 + total[16:32]).astype(I32) - 1
    block, lane = split_position(position, size)
    block_ref[...] = jnp.where(position >= 0, block, -1)
    lane_ref[...] = jnp.where(position >= 0, lane, 0)


def pair_kernel(counts_ref, own_ref, one_ref, two_ref, three_ref, slab_ref, out_ref, target_ref, sum_ref):
    _, live = list_offsets(counts_ref)
    size = group_size(live)
    targets = own_ref[...] + one_ref[...] + two_ref[...] + three_ref[...]
    pad = jnp.zeros((LANES - 8, LANES), F32)
    for half in range(2):
        rows = jnp.concatenate([targets[half * 8 : half * 8 + 8], pad], axis=0)
        target_ref[half * LANES : (half + 1) * LANES, :] = rows.T
    sum_ref[...] = jnp.zeros_like(sum_ref)
    column = lax.broadcasted_iota(I32, (16, LANES), 1)
    zero = jnp.zeros((16, LANES), F32)

    def tile_of_targets(turn, carry):
        begin = pl.multiple_of(turn * 16, 16)
        mine = target_ref[pl.ds(begin, 16), :]
        tx, ty, tz, ux, uy, uz = [jnp.broadcast_to(mine[:, k : k + 1], (16, LANES)) for k in range(6)]

        def block(b, acc):
            ax, ay, az, jx, jy, jz = acc
            source = slab_ref[pl.ds(pl.multiple_of(b * 8, 8), 8), :]
            sx, sy, sz, vx, vy, vz, mass = [source[k : k + 1] for k in range(7)]
            rx = sx - tx
            ry = sy - ty
            rz = sz - tz
            wx = vx - ux
            wy = vy - uy
            wz = vz - uz
            square = (rx * rx + softening_square) + ry * ry + rz * rz
            dot = rx * wx + ry * wy + rz * wz
            inverse = lax.rsqrt(square)
            inverse2 = inverse * inverse
            weight = (mass * inverse) * inverse2
            radial = (3.0 * dot) * inverse2
            return (
                ax + weight * rx,
                ay + weight * ry,
                az + weight * rz,
                jx + weight * (wx - radial * rx),
                jy + weight * (wy - radial * ry),
                jz + weight * (wz - radial * rz),
            )

        def blocks(turn8, acc):
            for k in range(8):
                acc = block(turn8 * 8 + k, acc)
            return acc

        acc = lax.fori_loop(0, BLOCKS // 8, blocks, (zero,) * 6)
        result = zero
        for k in range(6):
            result = jnp.where(column == k, jnp.sum(acc[k], axis=1, keepdims=True), result)
        sum_ref[pl.ds(begin, 16), :] = result
        return carry

    lax.fori_loop(0, (size + 15) >> 4, tile_of_targets, 0)
    for half in range(2):
        out_ref[half * 8 : half * 8 + 8, :] = sum_ref[half * LANES : (half + 1) * LANES, :].T[0:8]


def finish_kernel(counts_ref, block_ref, lane_ref, force_ref, state_ref, elapsed_ref, new_ref, active_ref):
    offsets, live = list_offsets(counts_ref)
    size = group_size(live)
    halves = jnp.where(size > LANES, 2, 1)
    my_list = lax.axis_index("x") * 2 + lax.axis_index("c")
    count = counts_ref[my_list]
    start = jnp.int32(0)
    for i in range(LISTS):
        start = jnp.where(my_list == i, offsets[i], start)
    row = lax.broadcasted_iota(I32, (8, LANES), 1)

    def gather(blocks, lanes):
        blocks = [jnp.broadcast_to(b, (8, LANES)) for b in blocks]
        lanes = [jnp.broadcast_to(b, (8, LANES)) for b in lanes]

        def step(turn, acc):
            acc = list(acc)
            for k in range(8):
                b = (turn * 8 + k) * (3 - halves)
                tile = force_ref[pl.ds(pl.multiple_of(b * 8, 8), 8), :]
                for n in range(len(acc)):
                    acc[n] = jnp.where(blocks[n] == b, take(tile, lanes[n]), acc[n])
            return tuple(acc)

        zero = jnp.zeros((8, LANES), F32)
        return lax.fori_loop(0, 8 * halves, step, (zero,) * len(blocks))

    for quarter in range(4):
        blocks = [block_ref[quarter * 4 + k : quarter * 4 + k + 1, :] for k in range(4)]
        lanes = [lane_ref[quarter * 4 + k : quarter * 4 + k + 1, :] for k in range(4)]
        found = gather(blocks, lanes)
        for k in range(4):
            part = slice((quarter * 4 + k) * LANES, (quarter * 4 + k + 1) * LANES)
            old = state_ref[:, part]
            step_time = elapsed_ref[:, part]
            force = found[k]
            half = step_time * 0.5
            twelfth = step_time * step_time / 12.0
            vel = old[3:6] + (old[6:9] + force[0:3]) * half + (old[9:12] - force[3:6]) * twelfth
            pos = old[0:3] + (old[3:6] + vel) * half + (old[6:9] - force[0:3]) * twelfth
            fresh = jnp.concatenate([pos, vel, force[0:6]], axis=0)
            new_ref[:, part] = jnp.where(blocks[k] >= 0, fresh, old)

    for quarter in range(4):
        span = slice(quarter * 512, quarter * 512 + 512)
        active_ref[:, span] = jnp.zeros((6, 512), F32)

        @pl.when(quarter * 512 < count)
        def _():
            blocks, lanes = [], []
            for k in range(4):
                slot = row + (quarter * 4 + k) * LANES
                b, lane = split_position(start + slot, size)
                blocks.append(jnp.where(slot < count, b, -1))
                lanes.append(lane)
            found = gather(blocks, lanes)
            for k in range(4):
                part = slice((quarter * 4 + k) * LANES, (quarter * 4 + k + 1) * LANES)
                active_ref[:, part] = found[k][0:6]


def exchange_y(part):
    return [lax.ppermute(part, "y", [(i, (i + k) % 4) for i in range(4)]) for k in range(1, 4)]


def spread(part):
    part = lax.all_to_all(part, ("x", "z"), 0, 0)
    return lax.all_gather(part, "c").reshape(1024, LANES)


def body(state, mass, elapsed, active_ids, active_count):
    mass = mass.reshape(1, SHARD)
    elapsed = elapsed.reshape(1, SHARD)
    ids = active_ids.reshape(1, CAP)
    packed = pl.pallas_call(
        pack_kernel,
        out_shape=jax.ShapeDtypeStruct((32, 16, LANES), F32),
        in_specs=[VMEM] * 4,
        out_specs=VMEM,
        name="pack",
    )(state, mass, elapsed, ids)
    slab = spread(packed)
    own = pl.pallas_call(
        extract_kernel,
        out_shape=jax.ShapeDtypeStruct((16, LANES), F32),
        in_specs=[SMEM, VMEM],
        out_specs=VMEM,
        name="extract",
    )(active_count, slab)
    others = exchange_y(own)
    blocks, lanes = pl.pallas_call(
        inverse_kernel,
        out_shape=[jax.ShapeDtypeStruct((16, LANES), I32)] * 2,
        in_specs=[SMEM, VMEM],
        out_specs=[VMEM, VMEM],
        name="inverse",
    )(active_count, slab)
    partial = pl.pallas_call(
        pair_kernel,
        out_shape=jax.ShapeDtypeStruct((16, LANES), F32),
        in_specs=[SMEM] + [VMEM] * 5,
        out_specs=VMEM,
        scratch_shapes=[pltpu.VMEM((256, LANES), F32), pltpu.VMEM((256, LANES), F32)],
        name="pairs",
    )(active_count, own, *others, slab)
    more = exchange_y(partial)
    force = partial + more[0] + more[1] + more[2]
    forces = spread(jnp.broadcast_to(force[None], (32, 16, LANES)))
    return pl.pallas_call(
        finish_kernel,
        out_shape=[
            jax.ShapeDtypeStruct((12, SHARD), F32),
            jax.ShapeDtypeStruct((6, CAP), F32),
        ],
        in_specs=[SMEM] + [VMEM] * 5,
        out_specs=[VMEM, VMEM],
        name="finish",
    )(active_count, blocks, lanes, forces, state, elapsed)


def solution(mesh):
    fine = Mesh(mesh.devices.reshape(4, 2, 4, 8), ("x", "c", "y", "z"))
    placed = (P(None, ("y", "z")), P(("y", "z")), P(("y", "z")), P(("x", "c")), P())
    return jax.shard_map(
        body,
        mesh=fine,
        in_specs=placed,
        out_specs=(P(None, ("y", "z")), P(None, ("x", "c"))),
        check_vma=False,
    )
```

```python
import jax
import jax.numpy as jnp
from jax import lax
from jax.experimental import pallas as pl
from jax.experimental.pallas import tpu as pltpu
from jax.sharding import Mesh, PartitionSpec as P

F32 = jnp.float32
I32 = jnp.int32
softening_square = 0.01
LISTS = 8
CAP = 2048
SHARD = 2048
GROUPS = 64
LANES = 128
BLOCKS = 128
SMEM = pl.BlockSpec(memory_space=pltpu.SMEM)
VMEM = pl.BlockSpec(memory_space=pltpu.VMEM)


def take(tile, index):
    return jnp.take_along_axis(tile, index, axis=1, mode="promise_in_bounds")


def list_offsets(counts_ref):
    offsets = [jnp.int32(0)]
    for i in range(LISTS):
        offsets.append(offsets[-1] + counts_ref[i])
    return offsets[:LISTS], offsets[LISTS]


def group_size(live):
    return lax.shift_right_logical(live + (GROUPS - 1), 6)


def split_position(position, size):
    group = jnp.floor((position.astype(F32) + 0.5) / size.astype(F32)).astype(I32)
    lane = position - group * size
    return group * 2 + (lane >> 7), lane & 127


def pack_kernel(state_ref, mass_ref, elapsed_ref, ids_ref, out_ref):
    eighth = lax.axis_index("x") * 2 + lax.axis_index("c")
    part = pl.ds(pl.multiple_of(eighth * 256, 256), 256)
    piece = pl.ds(pl.multiple_of(lax.axis_index("z") * 256, 256), 256)
    old = state_ref[:, part]
    step = elapsed_ref[:, part]
    half = step * step * 0.5
    sixth = half * step / 3.0
    pos = old[0:3] + old[3:6] * step + old[6:9] * half + old[9:12] * sixth
    vel = old[3:6] + old[6:9] * step + old[9:12] * half
    mass = mass_ref[:, part] * (1.0 / 65536.0)
    ids = ids_ref[:, piece].astype(F32)
    rows = jnp.concatenate([pos, vel, mass, ids], axis=0)
    both = jnp.concatenate([rows[:, :LANES], rows[:, LANES:]], axis=0)
    for peer in range(32):
        out_ref[peer] = both


def extract_kernel(counts_ref, slab_ref, out_ref):
    offsets, live = list_offsets(counts_ref)
    size = group_size(live)
    group = lax.axis_index("c") * 32 + lax.axis_index("x") * 8 + lax.axis_index("z")
    my_y = lax.axis_index("y")
    sub = lax.broadcasted_iota(I32, (8, LANES), 0)
    column = lax.broadcasted_iota(I32, (8, LANES), 1)

    def one_half(half):
        lane = column + half * LANES
        position = group * size + lane
        valid = (lane < size) & (position < live)
        which = jnp.zeros((8, LANES), I32)
        base = jnp.zeros((8, LANES), I32)
        for i in range(1, LISTS):
            after = position >= offsets[i]
            which = jnp.where(after, i, which)
            base = jnp.where(after, offsets[i], base)
        slot = jnp.where(valid, position - base, 0)
        block = (which & 1) * 64 + (which >> 1) * 16 + (slot >> 8) * 2 + ((slot >> 7) & 1)
        within = slot & 127
        found = jnp.zeros((8, LANES), F32)
        for v in range(16):
            tile = slab_ref[pl.ds(7 + 64 * v, 8, stride=8), :]
            found = jnp.where(block == v * 8 + sub, take(tile, within), found)
        star = jnp.broadcast_to(jnp.sum(found, axis=0, keepdims=True), (8, LANES)).astype(I32)
        mine = valid & ((star >> 14) == my_y)
        place = ((star >> 8) & 1) * 64 + ((star >> 9) & 3) * 16 + ((star >> 11) & 7) * 2 + ((star >> 7) & 1)
        place = jnp.where(mine, place, -1)
        inside = star & 127

        picked = jnp.zeros((8, LANES), F32)
        for b in range(BLOCKS):
            picked = jnp.where(place == b, take(slab_ref[b * 8 : b * 8 + 8, :], inside), picked)
        out_ref[half * 8 : half * 8 + 8, :] = jnp.where(sub < 6, picked, 0.0)

    one_half(0)
    out_ref[8:16, :] = jnp.zeros((8, LANES), F32)

    @pl.when(size > LANES)
    def _():
        one_half(1)


def plan_kernel(
    counts_ref, slab_ref, state_ref, elapsed_ref,
    number_ref, rank_ref, block_ref, lane_ref, known_ref, one_ref, two_ref,
):
    offsets, live = list_offsets(counts_ref)
    size = group_size(live)
    shard = lax.axis_index("y") * 8 + lax.axis_index("z")
    wide = 2 * LANES
    row16 = lax.broadcasted_iota(I32, (16, wide), 0)
    row128 = lax.broadcasted_iota(I32, (LANES, wide), 0)
    column = lax.broadcasted_iota(I32, (1, wide), 1)
    square_row = lax.broadcasted_iota(I32, (LANES, LANES), 0)
    square_column = lax.broadcasted_iota(I32, (LANES, LANES), 1)
    contract = (((1,), (1,)), ((), ()))
    total = jnp.zeros((32, LANES), F32)
    for i in range(LISTS):
        first = 7 + 64 * ((i & 1) * 8 + (i >> 1) * 2)

        def step(turn, acc):
            ids8 = slab_ref[pl.ds(first + 64 * turn, 8, stride=8), :].astype(I32)
            for k in range(0, 8, 2):
                ids = jnp.concatenate([ids8[k : k + 1], ids8[k + 1 : k + 2]], axis=1)
                slot = turn * 1024 + k * LANES + column
                mine = (slot < counts_ref[i]) & ((ids >> 11) == shard)
                high = jnp.where(mine, (ids >> 7) & 15, -1)
                low = ids & 127
                mark = offsets[i] + slot + 1
                here = row16 == high
                left = jnp.concatenate(
                    [
                        jnp.where(here, (mark >> 7).astype(F32), 0.0),
                        jnp.where(here, (mark & 127).astype(F32), 0.0),
                    ],
                    axis=0,
                ).astype(jnp.bfloat16)
                right = jnp.where(row128 == low, 1.0, 0.0).astype(jnp.bfloat16)
                acc = acc + lax.dot_general(left, right, contract, preferred_element_type=F32)
            return acc

        total = lax.fori_loop(0, (counts_ref[i] + 1023) >> 10, step, total)
    mark = (total[0:16] * 128.0 + total[16:32]).astype(I32)
    active = mark > 0
    flags = jnp.where(active, 1.0, 0.0).astype(jnp.bfloat16)
    upto = jnp.where(square_row <= square_column, 1.0, 0.0).astype(jnp.bfloat16)
    within = jnp.dot(flags, upto, preferred_element_type=F32)
    rows = jnp.broadcast_to(within[:, LANES - 1 :], (16, LANES)).astype(jnp.bfloat16)
    below = jnp.where(square_column[0:16, 0:16] < square_row[0:16, 0:16], 1.0, 0.0).astype(jnp.bfloat16)
    before = jnp.dot(below, rows, preferred_element_type=F32)
    rank = jnp.where(active, (within + before).astype(I32) - 1, -1)
    rank_ref[...] = rank
    number = jnp.sum(jnp.where(active, 1, 0))
    number_ref[0] = number
    row8 = lax.broadcasted_iota(I32, (8, LANES), 0)
    column8 = lax.broadcasted_iota(I32, (8, LANES), 1)

    def compact(turn, carry):
        sums = jnp.zeros((8, LANES), F32)
        for r in range(16):
            hit = jnp.where(rank[r : r + 1] - turn * LANES == square_row, 1.0, 0.0).astype(jnp.bfloat16)
            mine = mark[r : r + 1]
            facts = jnp.where(row8 == 0, mine >> 7, jnp.where(row8 == 1, mine & 127, jnp.where(row8 == 2, r, column8)))
            sums = sums + lax.dot_general(
                facts.astype(F32).astype(jnp.bfloat16), hit, contract, preferred_element_type=F32
            )
        mark_of = (sums[0:1] * 128.0 + sums[1:2]).astype(I32)
        block, lane = split_position(mark_of - 1, size)
        block_ref[pl.ds(turn, 1), :] = jnp.where(mark_of > 0, block, -1)
        lane_ref[pl.ds(turn, 1), :] = jnp.where(mark_of > 0, lane, 0)
        star_row = jnp.broadcast_to(sums[2:3], (8, LANES)).astype(I32)
        star_lane = jnp.broadcast_to(sums[3:4], (8, LANES)).astype(I32)
        head = jnp.zeros((8, LANES), F32)
        tail = jnp.zeros((8, LANES), F32)
        for r in range(16):
            part = slice(r * LANES, (r + 1) * LANES)
            here = star_row == r
            head = jnp.where(here, take(state_ref[0:8, part], star_lane), head)
            rest = jnp.concatenate(
                [state_ref[8:12, part], jnp.broadcast_to(elapsed_ref[:, part], (4, LANES))], axis=0
            )
            tail = jnp.where(here, take(rest, star_lane), tail)
        pos, vel = head[0:3], head[3:6]
        accel = jnp.concatenate([head[6:8], tail[0:1]], axis=0)
        jerk = tail[1:4]
        step_time = tail[4:5]
        half = step_time * 0.5
        twelfth = step_time * step_time / 12.0
        known_vel = vel + accel * half + jerk * twelfth
        known_pos = pos + (vel + known_vel) * half + accel * twelfth
        none = jnp.zeros((2, LANES), F32)
        wide3 = lambda value: jnp.broadcast_to(value, (3, LANES))
        begin = pl.ds(pl.multiple_of(turn * 8, 8), 8)
        known_ref[begin, :] = jnp.concatenate([known_pos, known_vel, none], axis=0)
        one_ref[begin, :] = jnp.concatenate([wide3(half * half - twelfth), wide3(half), none], axis=0)
        two_ref[begin, :] = jnp.concatenate([wide3(twelfth * half), wide3(twelfth), none], axis=0)
        return carry

    lax.fori_loop(0, (number + 127) >> 7, compact, 0)


def pair_kernel(counts_ref, own_ref, one_ref, two_ref, three_ref, slab_ref, out_ref, target_ref, sum_ref):
    _, live = list_offsets(counts_ref)
    size = group_size(live)
    targets = own_ref[...] + one_ref[...] + two_ref[...] + three_ref[...]
    pad = jnp.zeros((LANES - 8, LANES), F32)
    for half in range(2):
        rows = jnp.concatenate([targets[half * 8 : half * 8 + 8], pad], axis=0)
        target_ref[half * LANES : (half + 1) * LANES, :] = rows.T
    sum_ref[...] = jnp.zeros_like(sum_ref)
    column = lax.broadcasted_iota(I32, (16, LANES), 1)
    zero = jnp.zeros((16, LANES), F32)

    def tile_of_targets(turn, carry):
        begin = pl.multiple_of(turn * 16, 16)
        mine = target_ref[pl.ds(begin, 16), :]
        tx, ty, tz, ux, uy, uz = [jnp.broadcast_to(mine[:, k : k + 1], (16, LANES)) for k in range(6)]

        def block(b, acc):
            ax, ay, az, jx, jy, jz = acc
            source = slab_ref[pl.ds(pl.multiple_of(b * 8, 8), 8), :]
            sx, sy, sz, vx, vy, vz, mass = [source[k : k + 1] for k in range(7)]
            rx = sx - tx
            ry = sy - ty
            rz = sz - tz
            wx = vx - ux
            wy = vy - uy
            wz = vz - uz
            square = (rx * rx + softening_square) + ry * ry + rz * rz
            dot = rx * wx + ry * wy + rz * wz
            inverse = lax.rsqrt(square)
            inverse2 = inverse * inverse
            weight = (mass * inverse) * inverse2
            radial = (3.0 * dot) * inverse2
            return (
                ax + weight * rx,
                ay + weight * ry,
                az + weight * rz,
                jx + weight * (wx - radial * rx),
                jy + weight * (wy - radial * ry),
                jz + weight * (wz - radial * rz),
            )

        def blocks(turn8, acc):
            for k in range(8):
                acc = block(turn8 * 8 + k, acc)
            return acc

        acc = lax.fori_loop(0, BLOCKS // 8, blocks, (zero,) * 6)
        result = zero
        for k in range(6):
            result = jnp.where(column == k, jnp.sum(acc[k], axis=1, keepdims=True), result)
        sum_ref[pl.ds(begin, 16), :] = result
        return carry

    lax.fori_loop(0, (size + 15) >> 4, tile_of_targets, 0)
    for half in range(2):
        out_ref[half * 8 : half * 8 + 8, :] = sum_ref[half * LANES : (half + 1) * LANES, :].T[0:8]


def finish_kernel(
    counts_ref, number_ref, rank_ref, block_ref, lane_ref, known_ref, one_ref, two_ref,
    force_ref, state_ref, new_ref, active_ref,
):
    offsets, live = list_offsets(counts_ref)
    size = group_size(live)
    full = jnp.where(size > LANES, 1, 0)
    my_list = lax.axis_index("x") * 2 + lax.axis_index("c")
    count = counts_ref[my_list]
    start = jnp.int32(0)
    for i in range(LISTS):
        start = jnp.where(my_list == i, offsets[i], start)
    zero = jnp.zeros((8, LANES), F32)
    row = lax.broadcasted_iota(I32, (8, LANES), 1)

    blocks, lanes, firsts = [], [], []
    for b in range(CAP // LANES):
        slot = row + b * LANES
        block, lane = split_position(start + slot, size)
        blocks.append(jnp.where(slot < count, block, -1))
        lanes.append(lane)
        firsts.append(lax.div(start + b * LANES, size))

    def span(turn, acc):
        acc = list(acc)
        for b in range(CAP // LANES):
            tile = jnp.minimum(firsts[b] + (turn >> full), GROUPS - 1) * 2 + (turn & full)
            got = take(force_ref[pl.ds(pl.multiple_of(tile * 8, 8), 8), :], lanes[b])
            acc[b] = jnp.where(blocks[b] == tile, got, acc[b])
        return tuple(acc)

    spans = lax.div(jnp.int32(LANES - 1), size) + 2
    found = lax.fori_loop(0, spans << full, span, (zero,) * (CAP // LANES))
    for b in range(CAP // LANES):
        active_ref[:, b * LANES : (b + 1) * LANES] = found[b][0:6]

    new_ref[...] = state_ref[...]
    none = jnp.zeros((2, LANES), F32)

    def compact(turn, carry):
        block = jnp.broadcast_to(block_ref[pl.ds(turn, 1), :], (8, LANES))
        lane = jnp.broadcast_to(lane_ref[pl.ds(turn, 1), :], (8, LANES))

        def half(h, force):
            for g in range(GROUPS):
                tile = force_ref[pl.ds(pl.multiple_of(g * 16 + h * 8, 8), 8), :]
                force = jnp.where(block == g * 2 + h, take(tile, lane), force)
            return force

        force = lax.fori_loop(0, 1 + full, half, zero)
        begin = pl.ds(pl.multiple_of(turn * 8, 8), 8)
        accel = jnp.concatenate([force[0:3], force[0:3], none], axis=0)
        jerk = jnp.concatenate([force[3:6], force[3:6], none], axis=0)
        moved = known_ref[begin, :] + accel * one_ref[begin, :] - jerk * two_ref[begin, :]
        head = jnp.concatenate([moved[0:6], force[0:2]], axis=0)
        tail = jnp.concatenate([force[2:6], none, none], axis=0)
        for r in range(16):
            part = slice(r * LANES, (r + 1) * LANES)
            rank = jnp.broadcast_to(rank_ref[r : r + 1, :], (8, LANES))
            here = (rank >> 7) == turn
            place = rank & 127
            new_ref[0:8, part] = jnp.where(here, take(head, place), new_ref[0:8, part])
            new_ref[8:12, part] = jnp.where(here[0:4], take(tail, place)[0:4], new_ref[8:12, part])
        return carry

    lax.fori_loop(0, (number_ref[0] + 127) >> 7, compact, 0)


def exchange_y(part):
    return [lax.ppermute(part, "y", [(i, (i + k) % 4) for i in range(4)]) for k in range(1, 4)]


def spread(part):
    part = lax.all_to_all(part, ("x", "z"), 0, 0)
    return lax.all_gather(part, "c").reshape(1024, LANES)


def body(state, mass, elapsed, active_ids, active_count):
    mass = mass.reshape(1, SHARD)
    elapsed = elapsed.reshape(1, SHARD)
    ids = active_ids.reshape(1, CAP)
    packed = pl.pallas_call(
        pack_kernel,
        out_shape=jax.ShapeDtypeStruct((32, 16, LANES), F32),
        in_specs=[VMEM] * 4,
        out_specs=VMEM,
        name="pack",
    )(state, mass, elapsed, ids)
    slab = spread(packed)
    own = pl.pallas_call(
        extract_kernel,
        out_shape=jax.ShapeDtypeStruct((16, LANES), F32),
        in_specs=[SMEM, VMEM],
        out_specs=VMEM,
        name="extract",
    )(active_count, slab)
    others = exchange_y(own)
    square = jax.ShapeDtypeStruct((LANES, LANES), F32)
    plan = pl.pallas_call(
        plan_kernel,
        out_shape=[jax.ShapeDtypeStruct((1,), I32)]
        + [jax.ShapeDtypeStruct((16, LANES), I32)] * 3
        + [square] * 3,
        in_specs=[SMEM] + [VMEM] * 3,
        out_specs=[SMEM] + [VMEM] * 6,
        name="plan",
    )(active_count, slab, state, elapsed)
    partial = pl.pallas_call(
        pair_kernel,
        out_shape=jax.ShapeDtypeStruct((16, LANES), F32),
        in_specs=[SMEM] + [VMEM] * 5,
        out_specs=VMEM,
        scratch_shapes=[pltpu.VMEM((256, LANES), F32), pltpu.VMEM((256, LANES), F32)],
        name="pairs",
    )(active_count, own, *others, slab)
    more = exchange_y(partial)
    force = partial + more[0] + more[1] + more[2]
    forces = spread(jnp.broadcast_to(force[None], (32, 16, LANES)))
    return pl.pallas_call(
        finish_kernel,
        out_shape=[
            jax.ShapeDtypeStruct((12, SHARD), F32),
            jax.ShapeDtypeStruct((6, CAP), F32),
        ],
        in_specs=[SMEM] * 2 + [VMEM] * 8,
        out_specs=[VMEM, VMEM],
        name="finish",
    )(active_count, *plan, forces, state)


def solution(mesh):
    fine = Mesh(mesh.devices.reshape(4, 2, 4, 8), ("x", "c", "y", "z"))
    placed = (P(None, ("y", "z")), P(("y", "z")), P(("y", "z")), P(("x", "c")), P())
    return jax.shard_map(
        body,
        mesh=fine,
        in_specs=placed,
        out_specs=(P(None, ("y", "z")), P(None, ("x", "c"))),
        check_vma=False,
    )
```

```python
import jax
import jax.numpy as jnp
from jax import lax
from jax.experimental import pallas as pl
from jax.experimental.pallas import tpu as pltpu
from jax.sharding import Mesh, PartitionSpec as P

F32 = jnp.float32
I32 = jnp.int32
softening_square = 0.01
LISTS = 8
CAP = 2048
SHARD = 2048
GROUPS = 64
LANES = 128
SETS = 16
BLOCKS = 128
SMEM = pl.BlockSpec(memory_space=pltpu.SMEM)
VMEM = pl.BlockSpec(memory_space=pltpu.VMEM)


def take(tile, index):
    return jnp.take_along_axis(tile, index, axis=1, mode="promise_in_bounds")


def list_offsets(counts_ref):
    offsets = [jnp.int32(0)]
    for i in range(LISTS):
        offsets.append(offsets[-1] + counts_ref[i])
    return offsets[:LISTS], offsets[LISTS]


def group_size(live):
    return lax.shift_right_logical(live + (GROUPS - 1), 6)


def split_position(position, size):
    group = jnp.floor((position.astype(F32) + 0.5) / size.astype(F32)).astype(I32)
    lane = position - group * size
    return group * 2 + (lane >> 7), lane & 127


def pack_kernel(state_ref, mass_ref, elapsed_ref, ids_ref, out_ref):
    eighth = lax.axis_index("x") * 2 + lax.axis_index("c")
    part = pl.ds(pl.multiple_of(eighth * 256, 256), 256)
    piece = pl.ds(pl.multiple_of(lax.axis_index("z") * 256, 256), 256)
    old = state_ref[:, part]
    step = elapsed_ref[:, part]
    half = step * step * 0.5
    sixth = half * step / 3.0
    pos = old[0:3] + old[3:6] * step + old[6:9] * half + old[9:12] * sixth
    vel = old[3:6] + old[6:9] * step + old[9:12] * half
    mass = mass_ref[:, part] * (1.0 / 65536.0)
    ids = ids_ref[:, piece].astype(F32)
    rows = jnp.concatenate([pos, vel, mass, ids], axis=0)
    both = jnp.concatenate([rows[:, :LANES], rows[:, LANES:]], axis=0)
    for peer in range(32):
        out_ref[peer] = both


def extract_kernel(counts_ref, slab_ref, out_ref):
    offsets, live = list_offsets(counts_ref)
    size = group_size(live)
    group = lax.axis_index("c") * 32 + lax.axis_index("x") * 8 + lax.axis_index("z")
    my_y = lax.axis_index("y")
    sub = lax.broadcasted_iota(I32, (8, LANES), 0)
    column = lax.broadcasted_iota(I32, (8, LANES), 1)

    def one_half(half):
        lane = column + half * LANES
        position = group * size + lane
        valid = (lane < size) & (position < live)
        which = jnp.zeros((8, LANES), I32)
        base = jnp.zeros((8, LANES), I32)
        for i in range(1, LISTS):
            after = position >= offsets[i]
            which = jnp.where(after, i, which)
            base = jnp.where(after, offsets[i], base)
        slot = jnp.where(valid, position - base, 0)
        block = (which & 1) * 64 + (which >> 1) * 16 + (slot >> 8) * 2 + ((slot >> 7) & 1)
        within = slot & 127
        found = jnp.zeros((8, LANES), F32)
        for v in range(16):
            tile = slab_ref[pl.ds(7 + 64 * v, 8, stride=8), :]
            found = jnp.where(block == v * 8 + sub, take(tile, within), found)
        star = jnp.broadcast_to(jnp.sum(found, axis=0, keepdims=True), (8, LANES)).astype(I32)
        mine = valid & ((star >> 14) == my_y)
        place = ((star >> 8) & 1) * 64 + ((star >> 9) & 3) * 16 + ((star >> 11) & 7) * 2 + ((star >> 7) & 1)
        place = jnp.where(mine, place, -1)
        inside = star & 127

        picked = jnp.zeros((8, LANES), F32)
        for b in range(BLOCKS):
            picked = jnp.where(place == b, take(slab_ref[b * 8 : b * 8 + 8, :], inside), picked)
        out_ref[half * 8 : half * 8 + 8, :] = jnp.where(sub < 6, picked, 0.0)

    one_half(0)
    out_ref[8:16, :] = jnp.zeros((8, LANES), F32)

    @pl.when(size > LANES)
    def _():
        one_half(1)


def plan_kernel(
    counts_ref, slab_ref, state_ref, elapsed_ref,
    number_ref, rank_ref, block_ref, lane_ref, known_ref, one_ref, two_ref,
):
    offsets, live = list_offsets(counts_ref)
    size = group_size(live)
    shard = lax.axis_index("y") * 8 + lax.axis_index("z")
    wide = 2 * LANES
    row16 = lax.broadcasted_iota(I32, (16, wide), 0)
    row128 = lax.broadcasted_iota(I32, (LANES, wide), 0)
    column = lax.broadcasted_iota(I32, (1, wide), 1)
    square_row = lax.broadcasted_iota(I32, (LANES, LANES), 0)
    square_column = lax.broadcasted_iota(I32, (LANES, LANES), 1)
    contract = (((1,), (1,)), ((), ()))
    total = jnp.zeros((32, LANES), F32)
    for i in range(LISTS):
        first = 7 + 64 * ((i & 1) * 8 + (i >> 1) * 2)

        def step(turn, acc):
            ids8 = slab_ref[pl.ds(first + 64 * turn, 8, stride=8), :].astype(I32)
            for k in range(0, 8, 2):
                ids = jnp.concatenate([ids8[k : k + 1], ids8[k + 1 : k + 2]], axis=1)
                slot = turn * 1024 + k * LANES + column
                mine = (slot < counts_ref[i]) & ((ids >> 11) == shard)
                high = jnp.where(mine, (ids >> 7) & 15, -1)
                low = ids & 127
                mark = offsets[i] + slot + 1
                here = row16 == high
                left = jnp.concatenate(
                    [
                        jnp.where(here, (mark >> 7).astype(F32), 0.0),
                        jnp.where(here, (mark & 127).astype(F32), 0.0),
                    ],
                    axis=0,
                ).astype(jnp.bfloat16)
                right = jnp.where(row128 == low, 1.0, 0.0).astype(jnp.bfloat16)
                acc = acc + lax.dot_general(left, right, contract, preferred_element_type=F32)
            return acc

        total = lax.fori_loop(0, (counts_ref[i] + 1023) >> 10, step, total)
    mark = (total[0:16] * 128.0 + total[16:32]).astype(I32)
    active = mark > 0
    flags = jnp.where(active, 1.0, 0.0).astype(jnp.bfloat16)
    upto = jnp.where(square_row <= square_column, 1.0, 0.0).astype(jnp.bfloat16)
    within = jnp.dot(flags, upto, preferred_element_type=F32)
    rows = jnp.broadcast_to(within[:, LANES - 1 :], (16, LANES)).astype(jnp.bfloat16)
    below = jnp.where(square_column[0:16, 0:16] < square_row[0:16, 0:16], 1.0, 0.0).astype(jnp.bfloat16)
    before = jnp.dot(below, rows, preferred_element_type=F32)
    rank = jnp.where(active, (within + before).astype(I32) - 1, -1)
    rank_ref[...] = rank
    number = jnp.sum(jnp.where(active, 1, 0))
    number_ref[0] = number
    row8 = lax.broadcasted_iota(I32, (8, LANES), 0)
    column8 = lax.broadcasted_iota(I32, (8, LANES), 1)

    def compact(turn, carry):
        sums = jnp.zeros((8, LANES), F32)
        for r in range(16):
            hit = jnp.where(rank[r : r + 1] - turn * LANES == square_row, 1.0, 0.0).astype(jnp.bfloat16)
            mine = mark[r : r + 1]
            facts = jnp.where(row8 == 0, mine >> 7, jnp.where(row8 == 1, mine & 127, jnp.where(row8 == 2, r, column8)))
            sums = sums + lax.dot_general(
                facts.astype(F32).astype(jnp.bfloat16), hit, contract, preferred_element_type=F32
            )
        mark_of = (sums[0:1] * 128.0 + sums[1:2]).astype(I32)
        block, lane = split_position(mark_of - 1, size)
        block_ref[pl.ds(turn, 1), :] = jnp.where(mark_of > 0, block, -1)
        lane_ref[pl.ds(turn, 1), :] = jnp.where(mark_of > 0, lane, 0)
        star_row = jnp.broadcast_to(sums[2:3], (8, LANES)).astype(I32)
        star_lane = jnp.broadcast_to(sums[3:4], (8, LANES)).astype(I32)
        head = jnp.zeros((8, LANES), F32)
        tail = jnp.zeros((8, LANES), F32)
        for r in range(16):
            part = slice(r * LANES, (r + 1) * LANES)
            here = star_row == r
            head = jnp.where(here, take(state_ref[0:8, part], star_lane), head)
            rest = jnp.concatenate(
                [state_ref[8:12, part], jnp.broadcast_to(elapsed_ref[:, part], (4, LANES))], axis=0
            )
            tail = jnp.where(here, take(rest, star_lane), tail)
        pos, vel = head[0:3], head[3:6]
        accel = jnp.concatenate([head[6:8], tail[0:1]], axis=0)
        jerk = tail[1:4]
        step_time = tail[4:5]
        half = step_time * 0.5
        twelfth = step_time * step_time / 12.0
        known_vel = vel + accel * half + jerk * twelfth
        known_pos = pos + (vel + known_vel) * half + accel * twelfth
        none = jnp.zeros((2, LANES), F32)
        wide3 = lambda value: jnp.broadcast_to(value, (3, LANES))
        begin = pl.ds(pl.multiple_of(turn * 8, 8), 8)
        known_ref[begin, :] = jnp.concatenate([known_pos, known_vel, none], axis=0)
        one_ref[begin, :] = jnp.concatenate([wide3(half * half - twelfth), wide3(half), none], axis=0)
        two_ref[begin, :] = jnp.concatenate([wide3(twelfth * half), wide3(twelfth), none], axis=0)
        return carry

    lax.fori_loop(0, (number + 127) >> 7, compact, 0)


def pair_kernel(
    counts_ref, own_ref, one_ref, two_ref, three_ref, slab_ref, out_ref,
    splat_ref, source_ref, part_ref,
):
    _, live = list_offsets(counts_ref)
    size = group_size(live)
    column = lax.broadcasted_iota(I32, (8, LANES), 1)
    zero = jnp.zeros((8, LANES), F32)
    targets = own_ref[...] + one_ref[...] + two_ref[...] + three_ref[...]

    for v in range(SETS):
        for c in range(7):
            at = (c * SETS + v) * 8
            source_ref[at : at + 8, :] = slab_ref[pl.ds(v * 64 + c, 8, stride=8), :]

    def one_half(half):
        mine = targets[half * 8 : half * 8 + 8]
        for t in range(LANES):
            values = take(mine, jnp.full((8, LANES), t, I32))
            for c in range(6):
                at = (t * 6 + c) * 8
                splat_ref[at : at + 8, :] = jnp.broadcast_to(values[c : c + 1], (8, LANES))

        def four_targets(turn, carry):
            first = turn * 4
            sums = [zero] * 24
            for v in range(SETS):
                sx, sy, sz, vx, vy, vz, mass = [
                    source_ref[(c * SETS + v) * 8 : (c * SETS + v) * 8 + 8, :] for c in range(7)
                ]
                for t in range(4):
                    tx, ty, tz, ux, uy, uz = [
                        splat_ref[pl.ds(pl.multiple_of(((first + t) * 6 + c) * 8, 8), 8), :]
                        for c in range(6)
                    ]
                    rx = sx - tx
                    ry = sy - ty
                    rz = sz - tz
                    wx = vx - ux
                    wy = vy - uy
                    wz = vz - uz
                    square = (rx * rx + softening_square) + ry * ry + rz * rz
                    dot = rx * wx + ry * wy + rz * wz
                    inverse = lax.rsqrt(square)
                    inverse2 = inverse * inverse
                    weight = (mass * inverse) * inverse2
                    radial = (3.0 * dot) * inverse2
                    terms = (
                        rx, ry, rz,
                        wx - radial * rx, wy - radial * ry, wz - radial * rz,
                    )
                    for c in range(6):
                        sums[t * 6 + c] = sums[t * 6 + c] + weight * terms[c]
            for t in range(4):
                for c in range(6):
                    part_ref[pl.ds(pl.multiple_of((c * LANES + first + t) * 8, 8), 8), :] = sums[t * 6 + c]
            return carry

        count = jnp.minimum(size - half * LANES, LANES)
        lax.fori_loop(0, (count + 3) >> 2, four_targets, 0)
        rows = []
        for o in range(16):
            row = zero
            for c in range(6):
                first = (c * LANES + o * 8) * 8
                total = part_ref[pl.ds(first, 8, stride=8), :]
                for k in range(1, 8):
                    total = total + part_ref[pl.ds(first + k, 8, stride=8), :]
                row = jnp.where(column == c, jnp.sum(total, axis=1, keepdims=True), row)
            rows.append(row)
        out_ref[half * 8 : half * 8 + 8, :] = jnp.concatenate(rows, axis=0).T[0:8]

    one_half(0)

    @pl.when(size <= LANES)
    def _():
        out_ref[8:16, :] = zero

    @pl.when(size > LANES)
    def _():
        one_half(1)


def combine_kernel(own_ref, one_ref, two_ref, three_ref, out_ref):
    force = own_ref[...] + one_ref[...] + two_ref[...] + three_ref[...]
    for peer in range(32):
        out_ref[peer] = force


def finish_kernel(
    counts_ref, number_ref, rank_ref, block_ref, lane_ref, known_ref, one_ref, two_ref,
    force_ref, state_ref, new_ref, active_ref,
):
    offsets, live = list_offsets(counts_ref)
    size = group_size(live)
    full = jnp.where(size > LANES, 1, 0)
    my_list = lax.axis_index("x") * 2 + lax.axis_index("c")
    count = counts_ref[my_list]
    start = jnp.int32(0)
    for i in range(LISTS):
        start = jnp.where(my_list == i, offsets[i], start)
    zero = jnp.zeros((8, LANES), F32)
    row = lax.broadcasted_iota(I32, (8, LANES), 1)

    blocks, lanes, firsts = [], [], []
    for b in range(CAP // LANES):
        slot = row + b * LANES
        block, lane = split_position(start + slot, size)
        blocks.append(jnp.where(slot < count, block, -1))
        lanes.append(lane)
        firsts.append(lax.div(start + b * LANES, size))

    def span(turn, acc):
        acc = list(acc)
        for b in range(CAP // LANES):
            tile = jnp.minimum(firsts[b] + (turn >> full), GROUPS - 1) * 2 + (turn & full)
            got = take(force_ref[pl.ds(pl.multiple_of(tile * 8, 8), 8), :], lanes[b])
            acc[b] = jnp.where(blocks[b] == tile, got, acc[b])
        return tuple(acc)

    spans = lax.div(jnp.int32(LANES - 1), size) + 2
    found = lax.fori_loop(0, spans << full, span, (zero,) * (CAP // LANES))
    for b in range(CAP // LANES):
        active_ref[:, b * LANES : (b + 1) * LANES] = found[b][0:6]

    new_ref[...] = state_ref[...]
    none = jnp.zeros((2, LANES), F32)

    def compact(turn, carry):
        block = jnp.broadcast_to(block_ref[pl.ds(turn, 1), :], (8, LANES))
        lane = jnp.broadcast_to(lane_ref[pl.ds(turn, 1), :], (8, LANES))

        def half(h, force):
            for g in range(GROUPS):
                tile = force_ref[pl.ds(pl.multiple_of(g * 16 + h * 8, 8), 8), :]
                force = jnp.where(block == g * 2 + h, take(tile, lane), force)
            return force

        force = lax.fori_loop(0, 1 + full, half, zero)
        begin = pl.ds(pl.multiple_of(turn * 8, 8), 8)
        accel = jnp.concatenate([force[0:3], force[0:3], none], axis=0)
        jerk = jnp.concatenate([force[3:6], force[3:6], none], axis=0)
        moved = known_ref[begin, :] + accel * one_ref[begin, :] - jerk * two_ref[begin, :]
        head = jnp.concatenate([moved[0:6], force[0:2]], axis=0)
        tail = jnp.concatenate([force[2:6], none, none], axis=0)
        for r in range(16):
            part = slice(r * LANES, (r + 1) * LANES)
            rank = jnp.broadcast_to(rank_ref[r : r + 1, :], (8, LANES))
            here = (rank >> 7) == turn
            place = rank & 127
            new_ref[0:8, part] = jnp.where(here, take(head, place), new_ref[0:8, part])
            new_ref[8:12, part] = jnp.where(here[0:4], take(tail, place)[0:4], new_ref[8:12, part])
        return carry

    lax.fori_loop(0, (number_ref[0] + 127) >> 7, compact, 0)


def exchange_y(part):
    return [lax.ppermute(part, "y", [(i, (i + k) % 4) for i in range(4)]) for k in range(1, 4)]


def spread(part):
    part = lax.all_to_all(part, ("x", "z"), 0, 0)
    return lax.all_gather(part, "c").reshape(1024, LANES)


def in_vmem(*arrays):
    return [pltpu.with_memory_space_constraint(array, pltpu.VMEM) for array in arrays]


def body(state, mass, elapsed, active_ids, active_count):
    mass = mass.reshape(1, SHARD)
    elapsed = elapsed.reshape(1, SHARD)
    ids = active_ids.reshape(1, CAP)
    packed = pl.pallas_call(
        pack_kernel,
        out_shape=pltpu.VMEM((32, 16, LANES), F32),
        in_specs=[VMEM] * 4,
        out_specs=VMEM,
        name="pack",
    )(state, mass, elapsed, ids)
    slab = spread(packed)
    own = pl.pallas_call(
        extract_kernel,
        out_shape=pltpu.VMEM((16, LANES), F32),
        in_specs=[SMEM, VMEM],
        out_specs=VMEM,
        name="extract",
    )(active_count, *in_vmem(slab))
    others = exchange_y(own)
    square = pltpu.VMEM((LANES, LANES), F32)
    plan = pl.pallas_call(
        plan_kernel,
        out_shape=[jax.ShapeDtypeStruct((1,), I32)]
        + [pltpu.VMEM((16, LANES), I32)] * 3
        + [square] * 3,
        in_specs=[SMEM] + [VMEM] * 3,
        out_specs=[SMEM] + [VMEM] * 6,
        name="plan",
    )(active_count, *in_vmem(slab, state, elapsed))
    partial = pl.pallas_call(
        pair_kernel,
        out_shape=pltpu.VMEM((16, LANES), F32),
        in_specs=[SMEM] + [VMEM] * 5,
        out_specs=VMEM,
        scratch_shapes=[
            pltpu.VMEM((LANES * 6 * 8, LANES), F32),
            pltpu.VMEM((7 * SETS * 8, LANES), F32),
            pltpu.VMEM((6 * LANES * 8, LANES), F32),
        ],
        compiler_params=pltpu.CompilerParams(vmem_limit_bytes=24 * 2**20),
        name="pairs",
    )(active_count, *in_vmem(own, *others, slab))
    combined = pl.pallas_call(
        combine_kernel,
        out_shape=pltpu.VMEM((32, 16, LANES), F32),
        in_specs=[VMEM] * 4,
        out_specs=VMEM,
        name="combine",
    )(*in_vmem(partial, *exchange_y(partial)))
    forces = spread(combined)
    return pl.pallas_call(
        finish_kernel,
        out_shape=[
            jax.ShapeDtypeStruct((12, SHARD), F32),
            jax.ShapeDtypeStruct((6, CAP), F32),
        ],
        in_specs=[SMEM] * 2 + [VMEM] * 8,
        out_specs=[VMEM, VMEM],
        name="finish",
    )(active_count, plan[0], *in_vmem(*plan[1:], forces, state))


def solution(mesh):
    fine = Mesh(mesh.devices.reshape(4, 2, 4, 8), ("x", "c", "y", "z"))
    placed = (P(None, ("y", "z")), P(("y", "z")), P(("y", "z")), P(("x", "c")), P())
    return jax.shard_map(
        body,
        mesh=fine,
        in_specs=placed,
        out_specs=(P(None, ("y", "z")), P(None, ("x", "c"))),
        check_vma=False,
    )
```

```python
import jax
import jax.numpy as jnp
from jax import lax
from jax.experimental import pallas as pl
from jax.experimental.pallas import tpu as pltpu
from jax.sharding import Mesh, PartitionSpec as P

F32 = jnp.float32
I32 = jnp.int32
softening_square = 0.01
LISTS = 8
CAP = 2048
SHARD = 2048
GROUPS = 64
LANES = 128
SETS = 16
BLOCKS = 128
SMEM = pl.BlockSpec(memory_space=pltpu.SMEM)
VMEM = pl.BlockSpec(memory_space=pltpu.VMEM)


def take(tile, index):
    return jnp.take_along_axis(tile, index, axis=1, mode="promise_in_bounds")


def list_offsets(counts_ref):
    offsets = [jnp.int32(0)]
    for i in range(LISTS):
        offsets.append(offsets[-1] + counts_ref[i])
    return offsets[:LISTS], offsets[LISTS]


def at_list(offsets, wanted):
    start = jnp.int32(0)
    for i in range(LISTS):
        start = jnp.where(wanted == i, offsets[i], start)
    return start


def group_size(live):
    return lax.shift_right_logical(live + (GROUPS - 1), 6)


def split_position(position, size):
    group = jnp.floor((position.astype(F32) + 0.5) / size.astype(F32)).astype(I32)
    lane = position - group * size
    return group * 2 + (lane >> 7), lane & 127


def pack_kernel(state_ref, mass_ref, elapsed_ref, ids_ref, out_ref):
    eighth = lax.axis_index("x") * 2 + lax.axis_index("c")
    part = pl.ds(pl.multiple_of(eighth * 256, 256), 256)
    piece = pl.ds(pl.multiple_of(lax.axis_index("z") * 256, 256), 256)
    old = state_ref[:, part]
    step = elapsed_ref[:, part]
    half = step * step * 0.5
    sixth = half * step / 3.0
    pos = old[0:3] + old[3:6] * step + old[6:9] * half + old[9:12] * sixth
    vel = old[3:6] + old[6:9] * step + old[9:12] * half
    mass = mass_ref[:, part] * (1.0 / 65536.0)
    ids = ids_ref[:, piece].astype(F32)
    rows = jnp.concatenate([pos, vel, mass, ids], axis=0)
    both = jnp.concatenate([rows[:, :LANES], rows[:, LANES:]], axis=0)
    for peer in range(32):
        out_ref[peer] = both


def extract_kernel(counts_ref, mine_ref, other_ref, out_ref):
    offsets, live = list_offsets(counts_ref)
    size = group_size(live)
    core = lax.axis_index("c")
    group = core * 32 + lax.axis_index("x") * 8 + lax.axis_index("z")
    my_y = lax.axis_index("y")
    halves = (mine_ref, other_ref)
    sub = lax.broadcasted_iota(I32, (8, LANES), 0)
    column = lax.broadcasted_iota(I32, (8, LANES), 1)

    def one_half(half):
        lane = column + half * LANES
        position = group * size + lane
        valid = (lane < size) & (position < live)
        which = jnp.zeros((8, LANES), I32)
        base = jnp.zeros((8, LANES), I32)
        for i in range(1, LISTS):
            after = position >= offsets[i]
            which = jnp.where(after, i, which)
            base = jnp.where(after, offsets[i], base)
        slot = jnp.where(valid, position - base, 0)
        block = ((which & 1) ^ core) * 64 + (which >> 1) * 16 + (slot >> 7)
        within = slot & 127
        found = jnp.zeros((8, LANES), F32)
        for v in range(16):
            tile = halves[v >> 3][pl.ds(7 + 64 * (v & 7), 8, stride=8), :]
            found = jnp.where(block == v * 8 + sub, take(tile, within), found)
        star = jnp.broadcast_to(jnp.sum(found, axis=0, keepdims=True), (8, LANES)).astype(I32)
        mine = valid & ((star >> 14) == my_y)
        place = (((star >> 8) & 1) ^ core) * 64 + ((star >> 9) & 3) * 16 + ((star >> 11) & 7) * 2 + ((star >> 7) & 1)
        place = jnp.where(mine, place, -1)
        inside = star & 127
        picked = jnp.zeros((8, LANES), F32)
        for b in range(BLOCKS):
            tile = halves[b >> 6][(b & 63) * 8 : (b & 63) * 8 + 8, :]
            picked = jnp.where(place == b, take(tile, inside), picked)
        out_ref[half * 8 : half * 8 + 8, :] = jnp.where(sub < 6, picked, 0.0)

    one_half(0)
    out_ref[8:16, :] = jnp.zeros((8, LANES), F32)

    @pl.when(size > LANES)
    def _():
        one_half(1)


def plan_kernel(
    counts_ref, mine_ref, other_ref, state_ref, elapsed_ref,
    number_ref, rank_ref, block_ref, lane_ref, known_ref, one_ref, two_ref,
):
    offsets, live = list_offsets(counts_ref)
    size = group_size(live)
    shard = lax.axis_index("y") * 8 + lax.axis_index("z")
    wide = 2 * LANES
    row16 = lax.broadcasted_iota(I32, (16, wide), 0)
    row128 = lax.broadcasted_iota(I32, (LANES, wide), 0)
    column = lax.broadcasted_iota(I32, (1, wide), 1)
    square_row = lax.broadcasted_iota(I32, (LANES, LANES), 0)
    square_column = lax.broadcasted_iota(I32, (LANES, LANES), 1)
    contract = (((1,), (1,)), ((), ()))
    total = jnp.zeros((32, LANES), F32)
    for n in range(LISTS):
        i = (n & 6) + ((n & 1) ^ lax.axis_index("c"))
        count = counts_ref[i]
        start = at_list(offsets, i)
        half_ref = other_ref if n & 1 else mine_ref
        first = 7 + 64 * (n & 6)

        def step(turn, acc):
            ids8 = half_ref[pl.ds(first + 64 * turn, 8, stride=8), :].astype(I32)
            for k in range(0, 8, 2):
                ids = jnp.concatenate([ids8[k : k + 1], ids8[k + 1 : k + 2]], axis=1)
                slot = turn * 1024 + k * LANES + column
                mine = (slot < count) & ((ids >> 11) == shard)
                high = jnp.where(mine, (ids >> 7) & 15, -1)
                low = ids & 127
                mark = start + slot + 1
                here = row16 == high
                left = jnp.concatenate(
                    [
                        jnp.where(here, (mark >> 7).astype(F32), 0.0),
                        jnp.where(here, (mark & 127).astype(F32), 0.0),
                    ],
                    axis=0,
                ).astype(jnp.bfloat16)
                right = jnp.where(row128 == low, 1.0, 0.0).astype(jnp.bfloat16)
                acc = acc + lax.dot_general(left, right, contract, preferred_element_type=F32)
            return acc

        total = lax.fori_loop(0, (count + 1023) >> 10, step, total)
    mark = (total[0:16] * 128.0 + total[16:32]).astype(I32)
    active = mark > 0
    flags = jnp.where(active, 1.0, 0.0).astype(jnp.bfloat16)
    upto = jnp.where(square_row <= square_column, 1.0, 0.0).astype(jnp.bfloat16)
    within = jnp.dot(flags, upto, preferred_element_type=F32)
    rows = jnp.broadcast_to(within[:, LANES - 1 :], (16, LANES)).astype(jnp.bfloat16)
    below = jnp.where(square_column[0:16, 0:16] < square_row[0:16, 0:16], 1.0, 0.0).astype(jnp.bfloat16)
    before = jnp.dot(below, rows, preferred_element_type=F32)
    rank = jnp.where(active, (within + before).astype(I32) - 1, -1)
    rank_ref[...] = rank
    number = jnp.sum(jnp.where(active, 1, 0))
    number_ref[0] = number
    row8 = lax.broadcasted_iota(I32, (8, LANES), 0)
    column8 = lax.broadcasted_iota(I32, (8, LANES), 1)

    def compact(turn, carry):
        sums = jnp.zeros((8, LANES), F32)
        for r in range(16):
            hit = jnp.where(rank[r : r + 1] - turn * LANES == square_row, 1.0, 0.0).astype(jnp.bfloat16)
            mine = mark[r : r + 1]
            facts = jnp.where(row8 == 0, mine >> 7, jnp.where(row8 == 1, mine & 127, jnp.where(row8 == 2, r, column8)))
            sums = sums + lax.dot_general(
                facts.astype(F32).astype(jnp.bfloat16), hit, contract, preferred_element_type=F32
            )
        mark_of = (sums[0:1] * 128.0 + sums[1:2]).astype(I32)
        block, lane = split_position(mark_of - 1, size)
        block_ref[pl.ds(turn, 1), :] = jnp.where(mark_of > 0, block, -1)
        lane_ref[pl.ds(turn, 1), :] = jnp.where(mark_of > 0, lane, 0)
        star_row = jnp.broadcast_to(sums[2:3], (8, LANES)).astype(I32)
        star_lane = jnp.broadcast_to(sums[3:4], (8, LANES)).astype(I32)
        head = jnp.zeros((8, LANES), F32)
        tail = jnp.zeros((8, LANES), F32)
        for r in range(16):
            part = slice(r * LANES, (r + 1) * LANES)
            here = star_row == r
            head = jnp.where(here, take(state_ref[0:8, part], star_lane), head)
            rest = jnp.concatenate(
                [state_ref[8:12, part], jnp.broadcast_to(elapsed_ref[:, part], (4, LANES))], axis=0
            )
            tail = jnp.where(here, take(rest, star_lane), tail)
        pos, vel = head[0:3], head[3:6]
        accel = jnp.concatenate([head[6:8], tail[0:1]], axis=0)
        jerk = tail[1:4]
        step_time = tail[4:5]
        half = step_time * 0.5
        twelfth = step_time * step_time / 12.0
        known_vel = vel + accel * half + jerk * twelfth
        known_pos = pos + (vel + known_vel) * half + accel * twelfth
        none = jnp.zeros((2, LANES), F32)
        wide3 = lambda value: jnp.broadcast_to(value, (3, LANES))
        begin = pl.ds(pl.multiple_of(turn * 8, 8), 8)
        known_ref[begin, :] = jnp.concatenate([known_pos, known_vel, none], axis=0)
        one_ref[begin, :] = jnp.concatenate([wide3(half * half - twelfth), wide3(half), none], axis=0)
        two_ref[begin, :] = jnp.concatenate([wide3(twelfth * half), wide3(twelfth), none], axis=0)
        return carry

    lax.fori_loop(0, (number + 127) >> 7, compact, 0)


def pair_kernel(
    counts_ref, own_ref, one_ref, two_ref, three_ref, mine_ref, other_ref, out_ref,
    splat_ref, source_ref, part_ref,
):
    _, live = list_offsets(counts_ref)
    size = group_size(live)
    column = lax.broadcasted_iota(I32, (8, LANES), 1)
    zero = jnp.zeros((8, LANES), F32)
    halves = (mine_ref, other_ref)
    targets = own_ref[...] + one_ref[...] + two_ref[...] + three_ref[...]

    for v in range(SETS):
        for c in range(7):
            at = (c * SETS + v) * 8
            source_ref[at : at + 8, :] = halves[v >> 3][pl.ds((v & 7) * 64 + c, 8, stride=8), :]

    def one_half(half):
        mine = targets[half * 8 : half * 8 + 8]
        for t in range(LANES):
            values = take(mine, jnp.full((8, LANES), t, I32))
            for c in range(6):
                at = (t * 6 + c) * 8
                splat_ref[at : at + 8, :] = jnp.broadcast_to(values[c : c + 1], (8, LANES))

        def four_targets(turn, carry):
            first = turn * 4
            sums = [zero] * 24
            for v in range(SETS):
                sx, sy, sz, vx, vy, vz, mass = [
                    source_ref[(c * SETS + v) * 8 : (c * SETS + v) * 8 + 8, :] for c in range(7)
                ]
                for t in range(4):
                    tx, ty, tz, ux, uy, uz = [
                        splat_ref[pl.ds(pl.multiple_of(((first + t) * 6 + c) * 8, 8), 8), :]
                        for c in range(6)
                    ]
                    rx = sx - tx
                    ry = sy - ty
                    rz = sz - tz
                    wx = vx - ux
                    wy = vy - uy
                    wz = vz - uz
                    square = (rx * rx + softening_square) + ry * ry + rz * rz
                    dot = rx * wx + ry * wy + rz * wz
                    inverse = lax.rsqrt(square)
                    inverse2 = inverse * inverse
                    weight = (mass * inverse) * inverse2
                    radial = (3.0 * dot) * inverse2
                    terms = (
                        rx, ry, rz,
                        wx - radial * rx, wy - radial * ry, wz - radial * rz,
                    )
                    for c in range(6):
                        sums[t * 6 + c] = sums[t * 6 + c] + weight * terms[c]
            for t in range(4):
                for c in range(6):
                    part_ref[pl.ds(pl.multiple_of((c * LANES + first + t) * 8, 8), 8), :] = sums[t * 6 + c]
            return carry

        count = jnp.minimum(size - half * LANES, LANES)
        lax.fori_loop(0, (count + 3) >> 2, four_targets, 0)
        rows = []
        for o in range(16):
            row = zero
            for c in range(6):
                first = (c * LANES + o * 8) * 8
                total = part_ref[pl.ds(first, 8, stride=8), :]
                for k in range(1, 8):
                    total = total + part_ref[pl.ds(first + k, 8, stride=8), :]
                row = jnp.where(column == c, jnp.sum(total, axis=1, keepdims=True), row)
            rows.append(row)
        out_ref[half * 8 : half * 8 + 8, :] = jnp.concatenate(rows, axis=0).T[0:8]

    one_half(0)

    @pl.when(size <= LANES)
    def _():
        out_ref[8:16, :] = zero

    @pl.when(size > LANES)
    def _():
        one_half(1)


def combine_kernel(own_ref, one_ref, two_ref, three_ref, out_ref):
    force = own_ref[...] + one_ref[...] + two_ref[...] + three_ref[...]
    for peer in range(32):
        out_ref[peer] = force


def finish_kernel(
    counts_ref, number_ref, rank_ref, block_ref, lane_ref, known_ref, one_ref, two_ref,
    mine_ref, other_ref, state_ref, new_ref, active_ref,
):
    offsets, live = list_offsets(counts_ref)
    size = group_size(live)
    full = jnp.where(size > LANES, 1, 0)
    core = lax.axis_index("c")
    my_list = lax.axis_index("x") * 2 + core
    count = counts_ref[my_list]
    start = at_list(offsets, my_list)
    zero = jnp.zeros((8, LANES), F32)
    row = lax.broadcasted_iota(I32, (8, LANES), 1)

    blocks, lanes, firsts = [], [], []
    for b in range(CAP // LANES):
        slot = row + b * LANES
        block, lane = split_position(start + slot, size)
        blocks.append(jnp.where(slot < count, block, -1))
        lanes.append(lane)
        firsts.append(lax.div(start + b * LANES, size))

    def span(turn, acc):
        acc = list(acc)
        for b in range(CAP // LANES):
            tile = jnp.minimum(firsts[b] + (turn >> full), GROUPS - 1) * 2 + (turn & full)
            rows = pl.ds(pl.multiple_of((tile & 63) * 8, 8), 8)
            forces = jnp.where((tile >> 6) == core, mine_ref[rows, :], other_ref[rows, :])
            acc[b] = jnp.where(blocks[b] == tile, take(forces, lanes[b]), acc[b])
        return tuple(acc)

    spans = lax.div(jnp.int32(LANES - 1), size) + 2
    found = lax.fori_loop(0, spans << full, span, (zero,) * (CAP // LANES))
    for b in range(CAP // LANES):
        active_ref[:, b * LANES : (b + 1) * LANES] = found[b][0:6]

    new_ref[...] = state_ref[...]
    none = jnp.zeros((2, LANES), F32)

    def compact(turn, carry):
        block = jnp.broadcast_to(block_ref[pl.ds(turn, 1), :], (8, LANES)) ^ (core * 64)
        lane = jnp.broadcast_to(lane_ref[pl.ds(turn, 1), :], (8, LANES))

        def half(h, force):
            for g in range(GROUPS):
                half_ref = mine_ref if g < 32 else other_ref
                tile = half_ref[pl.ds(pl.multiple_of((g & 31) * 16 + h * 8, 8), 8), :]
                force = jnp.where(block == g * 2 + h, take(tile, lane), force)
            return force

        force = lax.fori_loop(0, 1 + full, half, zero)
        begin = pl.ds(pl.multiple_of(turn * 8, 8), 8)
        accel = jnp.concatenate([force[0:3], force[0:3], none], axis=0)
        jerk = jnp.concatenate([force[3:6], force[3:6], none], axis=0)
        moved = known_ref[begin, :] + accel * one_ref[begin, :] - jerk * two_ref[begin, :]
        head = jnp.concatenate([moved[0:6], force[0:2]], axis=0)
        tail = jnp.concatenate([force[2:6], none, none], axis=0)
        for r in range(16):
            part = slice(r * LANES, (r + 1) * LANES)
            rank = jnp.broadcast_to(rank_ref[r : r + 1, :], (8, LANES))
            here = (rank >> 7) == turn
            place = rank & 127
            new_ref[0:8, part] = jnp.where(here, take(head, place), new_ref[0:8, part])
            new_ref[8:12, part] = jnp.where(here[0:4], take(tail, place)[0:4], new_ref[8:12, part])
        return carry

    lax.fori_loop(0, (number_ref[0] + 127) >> 7, compact, 0)


def exchange_y(part):
    return [lax.ppermute(part, "y", [(i, (i + k) % 4) for i in range(4)]) for k in range(1, 4)]


def in_vmem(*arrays):
    return [pltpu.with_memory_space_constraint(array, pltpu.VMEM) for array in arrays]


def spread(part, *done):
    part = lax.all_to_all(part, ("x", "z"), 0, 0).reshape(512, LANES)
    part, *done = lax.optimization_barrier((part, *done))
    return in_vmem(part, lax.ppermute(part, "c", [(0, 1), (1, 0)])), done


def body(state, mass, elapsed, active_ids, active_count):
    mass = mass.reshape(1, SHARD)
    elapsed = elapsed.reshape(1, SHARD)
    ids = active_ids.reshape(1, CAP)
    packed = pl.pallas_call(
        pack_kernel,
        out_shape=pltpu.VMEM((32, 16, LANES), F32),
        in_specs=[VMEM] * 4,
        out_specs=VMEM,
        name="pack",
    )(state, mass, elapsed, ids)
    slab, _ = spread(packed)
    own = pl.pallas_call(
        extract_kernel,
        out_shape=pltpu.VMEM((16, LANES), F32),
        in_specs=[SMEM, VMEM, VMEM],
        out_specs=VMEM,
        name="extract",
    )(active_count, *slab)
    others = exchange_y(own)
    square = pltpu.VMEM((LANES, LANES), F32)
    plan = pl.pallas_call(
        plan_kernel,
        out_shape=[jax.ShapeDtypeStruct((1,), I32)]
        + [pltpu.VMEM((16, LANES), I32)] * 3
        + [square] * 3,
        in_specs=[SMEM] + [VMEM] * 4,
        out_specs=[SMEM] + [VMEM] * 6,
        name="plan",
    )(active_count, *slab, *in_vmem(state, elapsed))
    partial = pl.pallas_call(
        pair_kernel,
        out_shape=pltpu.VMEM((16, LANES), F32),
        in_specs=[SMEM] + [VMEM] * 6,
        out_specs=VMEM,
        scratch_shapes=[
            pltpu.VMEM((LANES * 6 * 8, LANES), F32),
            pltpu.VMEM((7 * SETS * 8, LANES), F32),
            pltpu.VMEM((6 * LANES * 8, LANES), F32),
        ],
        compiler_params=pltpu.CompilerParams(vmem_limit_bytes=24 * 2**20),
        name="pairs",
    )(active_count, *in_vmem(own, *others), *slab)
    combined = pl.pallas_call(
        combine_kernel,
        out_shape=pltpu.VMEM((32, 16, LANES), F32),
        in_specs=[VMEM] * 4,
        out_specs=VMEM,
        name="combine",
    )(*in_vmem(partial, *exchange_y(partial)))
    forces, plan = spread(combined, *plan)
    return pl.pallas_call(
        finish_kernel,
        out_shape=[
            jax.ShapeDtypeStruct((12, SHARD), F32),
            jax.ShapeDtypeStruct((6, CAP), F32),
        ],
        in_specs=[SMEM] * 2 + [VMEM] * 9,
        out_specs=[VMEM, VMEM],
        name="finish",
    )(active_count, plan[0], *in_vmem(*plan[1:]), *forces, *in_vmem(state))


def solution(mesh):
    fine = Mesh(mesh.devices.reshape(4, 2, 4, 8), ("x", "c", "y", "z"))
    placed = (P(None, ("y", "z")), P(("y", "z")), P(("y", "z")), P(("x", "c")), P())
    return jax.shard_map(
        body,
        mesh=fine,
        in_specs=placed,
        out_specs=(P(None, ("y", "z")), P(None, ("x", "c"))),
        check_vma=False,
    )
```

```python
import functools

import jax
import jax.numpy as jnp
from jax import lax
from jax.experimental import pallas as pl
from jax.experimental.pallas import tpu as pltpu
from jax.sharding import Mesh, PartitionSpec as P

F32 = jnp.float32
I32 = jnp.int32
softening_square = 0.01
LISTS = 8
CAP = 2048
SHARD = 2048
GROUPS = 64
LANES = 128
SETS = 16
BLOCKS = 128
SMEM = pl.BlockSpec(memory_space=pltpu.SMEM)
VMEM = pl.BlockSpec(memory_space=pltpu.VMEM)


def take(tile, index):
    return jnp.take_along_axis(tile, index, axis=1, mode="promise_in_bounds")


def list_offsets(counts_ref):
    offsets = [jnp.int32(0)]
    for i in range(LISTS):
        offsets.append(offsets[-1] + counts_ref[i])
    return offsets[:LISTS], offsets[LISTS]


def at_list(offsets, wanted):
    start = jnp.int32(0)
    for i in range(LISTS):
        start = jnp.where(wanted == i, offsets[i], start)
    return start


def group_size(live):
    return lax.shift_right_logical(live + (GROUPS - 1), 6)


def split_position(position, size):
    group = jnp.floor((position.astype(F32) + 0.5) / size.astype(F32)).astype(I32)
    lane = position - group * size
    return group * 2 + (lane >> 7), lane & 127


def pack_kernel(state_ref, mass_ref, elapsed_ref, ids_ref, out_ref):
    eighth = lax.axis_index("x") * 2 + lax.axis_index("c")
    part = pl.ds(pl.multiple_of(eighth * 256, 256), 256)
    piece = pl.ds(pl.multiple_of(lax.axis_index("z") * 256, 256), 256)
    old = state_ref[:, part]
    step = elapsed_ref[:, part]
    half = step * step * 0.5
    sixth = half * step / 3.0
    pos = old[0:3] + old[3:6] * step + old[6:9] * half + old[9:12] * sixth
    vel = old[3:6] + old[6:9] * step + old[9:12] * half
    mass = mass_ref[:, part] * (1.0 / 65536.0)
    ids = ids_ref[:, piece].astype(F32)
    rows = jnp.concatenate([pos, vel, mass, ids], axis=0)
    both = jnp.concatenate([rows[:, :LANES], rows[:, LANES:]], axis=0)
    for peer in range(32):
        out_ref[peer] = both


def extract_kernel(counts_ref, mine_ref, other_ref, out_ref):
    offsets, live = list_offsets(counts_ref)
    size = group_size(live)
    core = lax.axis_index("c")
    group = core * 32 + lax.axis_index("z") * 4 + lax.axis_index("x")
    my_y = lax.axis_index("y")
    halves = (mine_ref, other_ref)
    sub = lax.broadcasted_iota(I32, (8, LANES), 0)
    column = lax.broadcasted_iota(I32, (8, LANES), 1)

    def one_half(half):
        lane = column + half * LANES
        position = group * size + lane
        valid = (lane < size) & (position < live)
        which = jnp.zeros((8, LANES), I32)
        base = jnp.zeros((8, LANES), I32)
        for i in range(1, LISTS):
            after = position >= offsets[i]
            which = jnp.where(after, i, which)
            base = jnp.where(after, offsets[i], base)
        slot = jnp.where(valid, position - base, 0)
        block = ((which & 1) ^ core) * 64 + (slot >> 8) * 8 + (which >> 1) * 2 + ((slot >> 7) & 1)
        within = slot & 127
        found = jnp.zeros((8, LANES), F32)
        for v in range(16):
            tile = halves[v >> 3][pl.ds(7 + 64 * (v & 7), 8, stride=8), :]
            found = jnp.where(block == v * 8 + sub, take(tile, within), found)
        star = jnp.broadcast_to(jnp.sum(found, axis=0, keepdims=True), (8, LANES)).astype(I32)
        mine = valid & ((star >> 14) == my_y)
        place = (((star >> 8) & 1) ^ core) * 64 + ((star >> 11) & 7) * 8 + ((star >> 9) & 3) * 2 + ((star >> 7) & 1)
        place = jnp.where(mine, place, -1)
        inside = star & 127
        picked = jnp.zeros((8, LANES), F32)
        for b in range(BLOCKS):
            tile = halves[b >> 6][(b & 63) * 8 : (b & 63) * 8 + 8, :]
            picked = jnp.where(place == b, take(tile, inside), picked)
        out_ref[half * 8 : half * 8 + 8, :] = jnp.where(sub < 6, picked, 0.0)

    one_half(0)
    out_ref[8:16, :] = jnp.zeros((8, LANES), F32)

    @pl.when(size > LANES)
    def _():
        one_half(1)


def plan_kernel(
    counts_ref, mine_ref, other_ref, state_ref, elapsed_ref,
    number_ref, first_ref, rank_ref, block_ref, lane_ref, slot_block_ref, slot_lane_ref, known_ref, one_ref, two_ref,
):
    offsets, live = list_offsets(counts_ref)
    size = group_size(live)
    shard = lax.axis_index("y") * 8 + lax.axis_index("z")
    wide = 2 * LANES
    row16 = lax.broadcasted_iota(I32, (16, wide), 0)
    row128 = lax.broadcasted_iota(I32, (LANES, wide), 0)
    column = lax.broadcasted_iota(I32, (1, wide), 1)
    square_row = lax.broadcasted_iota(I32, (LANES, LANES), 0)
    square_column = lax.broadcasted_iota(I32, (LANES, LANES), 1)
    contract = (((1,), (1,)), ((), ()))

    my_list = lax.axis_index("x") * 2 + lax.axis_index("c")
    start = at_list(offsets, my_list)
    slots = lax.broadcasted_iota(I32, (16, LANES), 0) * LANES + lax.broadcasted_iota(I32, (16, LANES), 1)
    block, lane = split_position(start + slots, size)
    slot_block_ref[...] = jnp.where(slots < counts_ref[my_list], block, -1)
    slot_lane_ref[...] = lane
    for b in range(CAP // LANES):
        first_ref[b] = lax.div(start + b * LANES, size)
    first_ref[CAP // LANES] = lax.div(jnp.int32(LANES - 1), size) + 2

    total = jnp.zeros((32, LANES), F32)
    for n in range(LISTS):
        i = (n & 6) + ((n & 1) ^ lax.axis_index("c"))
        count = counts_ref[i]
        start = at_list(offsets, i)
        half_ref = other_ref if n & 1 else mine_ref
        first = 7 + 8 * (n & 6)

        def step(turn, acc):
            even, odd = [
                half_ref[pl.ds(first + 8 * k + 256 * turn, 4, stride=64), :].astype(I32) for k in range(2)
            ]
            for k in range(0, 8, 2):
                ids = jnp.concatenate([even[k // 2 : k // 2 + 1], odd[k // 2 : k // 2 + 1]], axis=1)
                slot = turn * 1024 + k * LANES + column
                mine = (slot < count) & ((ids >> 11) == shard)
                high = jnp.where(mine, (ids >> 7) & 15, -1)
                low = ids & 127
                mark = start + slot + 1
                here = row16 == high
                left = jnp.concatenate(
                    [
                        jnp.where(here, (mark >> 7).astype(F32), 0.0),
                        jnp.where(here, (mark & 127).astype(F32), 0.0),
                    ],
                    axis=0,
                ).astype(jnp.bfloat16)
                right = jnp.where(row128 == low, 1.0, 0.0).astype(jnp.bfloat16)
                acc = acc + lax.dot_general(left, right, contract, preferred_element_type=F32)
            return acc

        total = lax.fori_loop(0, (count + 1023) >> 10, step, total)
    mark = (total[0:16] * 128.0 + total[16:32]).astype(I32)
    active = mark > 0
    flags = jnp.where(active, 1.0, 0.0).astype(jnp.bfloat16)
    upto = jnp.where(square_row <= square_column, 1.0, 0.0).astype(jnp.bfloat16)
    within = jnp.dot(flags, upto, preferred_element_type=F32)
    rows = jnp.broadcast_to(within[:, LANES - 1 :], (16, LANES)).astype(jnp.bfloat16)
    below = jnp.where(square_column[0:16, 0:16] < square_row[0:16, 0:16], 1.0, 0.0).astype(jnp.bfloat16)
    before = jnp.dot(below, rows, preferred_element_type=F32)
    rank = jnp.where(active, (within + before).astype(I32) - 1, -1)
    rank_ref[...] = rank
    number = jnp.sum(jnp.where(active, 1, 0))
    number_ref[0] = number
    row8 = lax.broadcasted_iota(I32, (8, LANES), 0)
    column8 = lax.broadcasted_iota(I32, (8, LANES), 1)

    def compact(turn, carry):
        sums = jnp.zeros((8, LANES), F32)
        for r in range(16):
            hit = jnp.where(rank[r : r + 1] - turn * LANES == square_row, 1.0, 0.0).astype(jnp.bfloat16)
            mine = mark[r : r + 1]
            facts = jnp.where(row8 == 0, mine >> 7, jnp.where(row8 == 1, mine & 127, jnp.where(row8 == 2, r, column8)))
            sums = sums + lax.dot_general(
                facts.astype(F32).astype(jnp.bfloat16), hit, contract, preferred_element_type=F32
            )
        mark_of = (sums[0:1] * 128.0 + sums[1:2]).astype(I32)
        block, lane = split_position(mark_of - 1, size)
        block_ref[pl.ds(turn, 1), :] = jnp.where(mark_of > 0, block, -1)
        lane_ref[pl.ds(turn, 1), :] = jnp.where(mark_of > 0, lane, 0)
        star_row = jnp.broadcast_to(sums[2:3], (8, LANES)).astype(I32)
        star_lane = jnp.broadcast_to(sums[3:4], (8, LANES)).astype(I32)
        head = jnp.zeros((8, LANES), F32)
        tail = jnp.zeros((8, LANES), F32)
        for r in range(16):
            part = slice(r * LANES, (r + 1) * LANES)
            here = star_row == r
            head = jnp.where(here, take(state_ref[0:8, part], star_lane), head)
            rest = jnp.concatenate(
                [state_ref[8:12, part], jnp.broadcast_to(elapsed_ref[:, part], (4, LANES))], axis=0
            )
            tail = jnp.where(here, take(rest, star_lane), tail)
        pos, vel = head[0:3], head[3:6]
        accel = jnp.concatenate([head[6:8], tail[0:1]], axis=0)
        jerk = tail[1:4]
        step_time = tail[4:5]
        half = step_time * 0.5
        twelfth = step_time * step_time / 12.0
        known_vel = vel + accel * half + jerk * twelfth
        known_pos = pos + (vel + known_vel) * half + accel * twelfth
        none = jnp.zeros((2, LANES), F32)
        wide3 = lambda value: jnp.broadcast_to(value, (3, LANES))
        begin = pl.ds(pl.multiple_of(turn * 8, 8), 8)
        known_ref[begin, :] = jnp.concatenate([known_pos, known_vel, none], axis=0)
        one_ref[begin, :] = jnp.concatenate([wide3(half * half - twelfth), wide3(half), none], axis=0)
        two_ref[begin, :] = jnp.concatenate([wide3(twelfth * half), wide3(twelfth), none], axis=0)
        return carry

    lax.fori_loop(0, ((number + 255) >> 8) * 2, compact, 0)


def pair_kernel(
    counts_ref, own_ref, one_ref, two_ref, three_ref, mine_ref, other_ref, out_ref,
    splat_ref, source_ref, part_ref,
):
    _, live = list_offsets(counts_ref)
    size = group_size(live)
    column = lax.broadcasted_iota(I32, (8, LANES), 1)
    zero = jnp.zeros((8, LANES), F32)
    halves = (mine_ref, other_ref)
    targets = own_ref[...] + one_ref[...] + two_ref[...] + three_ref[...]

    for v in range(SETS):
        for c in range(7):
            at = (c * SETS + v) * 8
            source_ref[at : at + 8, :] = halves[v >> 3][pl.ds((v & 7) * 64 + c, 8, stride=8), :]

    def one_half(half):
        mine = targets[half * 8 : half * 8 + 8]
        for t in range(LANES):
            values = take(mine, jnp.full((8, LANES), t, I32))
            for c in range(6):
                at = (t * 6 + c) * 8
                splat_ref[at : at + 8, :] = jnp.broadcast_to(values[c : c + 1], (8, LANES))

        def four_targets(turn, carry):
            first = turn * 4
            sums = [zero] * 24
            for v in range(SETS):
                sx, sy, sz, vx, vy, vz, mass = [
                    source_ref[(c * SETS + v) * 8 : (c * SETS + v) * 8 + 8, :] for c in range(7)
                ]
                for t in range(4):
                    tx, ty, tz, ux, uy, uz = [
                        splat_ref[pl.ds(pl.multiple_of(((first + t) * 6 + c) * 8, 8), 8), :]
                        for c in range(6)
                    ]
                    rx = sx - tx
                    ry = sy - ty
                    rz = sz - tz
                    wx = vx - ux
                    wy = vy - uy
                    wz = vz - uz
                    square = (rx * rx + softening_square) + ry * ry + rz * rz
                    dot = rx * wx + ry * wy + rz * wz
                    inverse = lax.rsqrt(square)
                    inverse2 = inverse * inverse
                    weight = (mass * inverse) * inverse2
                    radial = (3.0 * dot) * inverse2
                    terms = (
                        rx, ry, rz,
                        wx - radial * rx, wy - radial * ry, wz - radial * rz,
                    )
                    for c in range(6):
                        sums[t * 6 + c] = sums[t * 6 + c] + weight * terms[c]
            for t in range(4):
                for c in range(6):
                    part_ref[pl.ds(pl.multiple_of((c * LANES + first + t) * 8, 8), 8), :] = sums[t * 6 + c]
            return carry

        count = jnp.minimum(size - half * LANES, LANES)
        lax.fori_loop(0, (count + 3) >> 2, four_targets, 0)
        rows = []
        for o in range(16):
            row = zero
            for c in range(6):
                first = (c * LANES + o * 8) * 8
                total = part_ref[pl.ds(first, 8, stride=8), :]
                for k in range(1, 8):
                    total = total + part_ref[pl.ds(first + k, 8, stride=8), :]
                row = jnp.where(column == c, jnp.sum(total, axis=1, keepdims=True), row)
            rows.append(row)
        out_ref[half * 8 : half * 8 + 8, :] = jnp.concatenate(rows, axis=0).T[0:8]

    one_half(0)

    @pl.when(size <= LANES)
    def _():
        out_ref[8:16, :] = zero

    @pl.when(size > LANES)
    def _():
        one_half(1)


def combine_kernel(own_ref, one_ref, two_ref, three_ref, out_ref, rest_ref):
    force = own_ref[...] + one_ref[...] + two_ref[...] + three_ref[...]
    for peer in range(32):
        out_ref[peer] = force[0:8]
    rest_ref[...] = force[8:16]


def finish_kernel(
    half, number_ref, first_ref, rank_ref, block_ref, lane_ref, slot_block_ref, slot_lane_ref, known_ref, one_ref, two_ref,
    mine_ref, other_ref, state_ref, *refs,
):
    new_ref, active_ref = refs[-2:]
    core = lax.axis_index("c")
    zero = jnp.zeros((8, LANES), F32)

    def wide(row):
        return jnp.broadcast_to(row, (8, LANES))

    def group_of(block):
        return jnp.where((block & 1) == half, block >> 1, -1)

    wanted = [group_of(wide(slot_block_ref[b : b + 1, :])) for b in range(CAP // LANES)]
    lanes = [wide(slot_lane_ref[b : b + 1, :]) for b in range(CAP // LANES)]
    firsts = [first_ref[b] for b in range(CAP // LANES)]

    def span(turn, acc):
        acc = list(acc)
        for b in range(CAP // LANES):
            group = jnp.minimum(firsts[b] + turn, GROUPS - 1)
            rows = pl.ds(pl.multiple_of((group & 31) * 8, 8), 8)
            forces = jnp.where((group >> 5) == core, mine_ref[rows, :], other_ref[rows, :])
            acc[b] = jnp.where(wanted[b] == group, take(forces, lanes[b]), acc[b])
        return tuple(acc)

    found = lax.fori_loop(0, first_ref[CAP // LANES], span, (zero,) * (CAP // LANES))
    for b in range(CAP // LANES):
        part = slice(b * LANES, (b + 1) * LANES)
        if half == 0:
            active_ref[:, part] = found[b][0:6]
        else:
            active_ref[:, part] = jnp.where(wanted[b][0:6] >= 0, found[b][0:6], refs[0][:, part])

    new_ref[...] = state_ref[...]
    none = jnp.zeros((2, LANES), F32)

    def moved(turn):
        group = group_of(wide(block_ref[pl.ds(turn, 1), :]))
        lane = wide(lane_ref[pl.ds(turn, 1), :])
        seen = group ^ (core * 32)
        force = zero
        for g in range(GROUPS):
            half_ref = mine_ref if g < 32 else other_ref
            force = jnp.where(seen == g, take(half_ref[(g & 31) * 8 : (g & 31) * 8 + 8, :], lane), force)
        begin = pl.ds(pl.multiple_of(turn * 8, 8), 8)
        accel = jnp.concatenate([force[0:3], force[0:3], none], axis=0)
        jerk = jnp.concatenate([force[3:6], force[3:6], none], axis=0)
        place = known_ref[begin, :] + accel * one_ref[begin, :] - jerk * two_ref[begin, :]
        head = jnp.concatenate([place[0:6], force[0:2]], axis=0)
        flag = jnp.where(group[0:4] >= 0, 1.0, 0.0)
        return head, jnp.concatenate([force[2:6], flag], axis=0)

    def compact(turn, carry):
        tiles = [moved(turn * 2), moved(turn * 2 + 1)]
        for r in range(16):
            part = slice(r * LANES, (r + 1) * LANES)
            rank = wide(rank_ref[r : r + 1, :])
            place = rank & 127
            top, bottom = new_ref[0:8, part], new_ref[8:12, part]
            for k, (head, tail) in enumerate(tiles):
                got = take(tail, place)
                here = (rank >> 7) == turn * 2 + k
                if half == 1:
                    here = here & (wide(got[7:8]) > 0.5)
                top = jnp.where(here, take(head, place), top)
                bottom = jnp.where(here[0:4], got[0:4], bottom)
            new_ref[0:8, part] = top
            new_ref[8:12, part] = bottom
        return carry

    lax.fori_loop(0, (number_ref[0] + 255) >> 8, compact, 0)


def exchange_y(part):
    return [lax.ppermute(part, "y", [(i, (i + k) % 4) for i in range(4)]) for k in range(1, 4)]


def in_vmem(*arrays):
    return [pltpu.with_memory_space_constraint(array, pltpu.VMEM) for array in arrays]


def spread(part, *done):
    part = lax.all_to_all(part, ("z", "x"), 0, 0).reshape(-1, LANES)
    part, *done = lax.optimization_barrier((part, *done))
    return in_vmem(part, lax.ppermute(part, "c", [(0, 1), (1, 0)])), done


def finish(half, plan, forces, state, *rest):
    return pl.pallas_call(
        functools.partial(finish_kernel, half),
        out_shape=[
            jax.ShapeDtypeStruct((12, SHARD), F32),
            jax.ShapeDtypeStruct((6, CAP), F32),
        ],
        in_specs=[SMEM] * 2 + [VMEM] * (11 + len(rest)),
        out_specs=[VMEM, VMEM],
        name="finish",
    )(*plan[:2], *in_vmem(*plan[2:]), *forces, *in_vmem(state, *rest))


def body(state, mass, elapsed, active_ids, active_count):
    mass = mass.reshape(1, SHARD)
    elapsed = elapsed.reshape(1, SHARD)
    ids = active_ids.reshape(1, CAP)
    packed = pl.pallas_call(
        pack_kernel,
        out_shape=pltpu.VMEM((32, 16, LANES), F32),
        in_specs=[VMEM] * 4,
        out_specs=VMEM,
        name="pack",
    )(state, mass, elapsed, ids)
    slab, _ = spread(packed)
    own = pl.pallas_call(
        extract_kernel,
        out_shape=pltpu.VMEM((16, LANES), F32),
        in_specs=[SMEM, VMEM, VMEM],
        out_specs=VMEM,
        name="extract",
    )(active_count, *slab)
    others = exchange_y(own)
    square = pltpu.VMEM((LANES, LANES), F32)
    plan = pl.pallas_call(
        plan_kernel,
        out_shape=[jax.ShapeDtypeStruct((1,), I32), jax.ShapeDtypeStruct((CAP // LANES + 1,), I32)]
        + [pltpu.VMEM((16, LANES), I32)] * 5
        + [square] * 3,
        in_specs=[SMEM] + [VMEM] * 4,
        out_specs=[SMEM] * 2 + [VMEM] * 8,
        name="plan",
    )(active_count, *slab, *in_vmem(state, elapsed))
    partial = pl.pallas_call(
        pair_kernel,
        out_shape=pltpu.VMEM((16, LANES), F32),
        in_specs=[SMEM] + [VMEM] * 6,
        out_specs=VMEM,
        scratch_shapes=[
            pltpu.VMEM((LANES * 6 * 8, LANES), F32),
            pltpu.VMEM((7 * SETS * 8, LANES), F32),
            pltpu.VMEM((6 * LANES * 8, LANES), F32),
        ],
        compiler_params=pltpu.CompilerParams(vmem_limit_bytes=24 * 2**20),
        name="pairs",
    )(active_count, *in_vmem(own, *others), *slab)
    combined, rest = pl.pallas_call(
        combine_kernel,
        out_shape=[pltpu.VMEM((32, 8, LANES), F32), jax.ShapeDtypeStruct((8, LANES), F32)],
        in_specs=[VMEM] * 4,
        out_specs=[VMEM] * 2,
        name="combine",
    )(*in_vmem(partial, *exchange_y(partial)))
    turns = (group_size(jnp.sum(active_count)) > LANES).astype(I32)
    forces, (turns, *plan) = spread(combined, turns, *plan)
    outputs = finish(0, plan, forces, state)

    def more(carry):
        turn, new_state, active_force = carry
        forces, _ = spread(jnp.broadcast_to(rest[None], (32, 8, LANES)))
        return (turn + 1, *finish(1, plan, forces, new_state, active_force))

    return lax.while_loop(lambda carry: carry[0] < turns, more, (jnp.int32(0), *outputs))[1:]


def solution(mesh):
    fine = Mesh(mesh.devices.reshape(4, 2, 4, 8), ("x", "c", "y", "z"))
    placed = (P(None, ("y", "z")), P(("y", "z")), P(("y", "z")), P(("x", "c")), P())
    return jax.shard_map(
        body,
        mesh=fine,
        in_specs=placed,
        out_specs=(P(None, ("y", "z")), P(None, ("x", "c"))),
        check_vma=False,
    )
```

```python
import functools

import jax
import jax.numpy as jnp
from jax import lax
from jax.experimental import pallas as pl
from jax.experimental.pallas import tpu as pltpu
from jax.sharding import Mesh, PartitionSpec as P

F32 = jnp.float32
I32 = jnp.int32
softening_square = 0.01
LISTS = 8
CAP = 2048
SHIFT = 5
SHARD = 2048
GROUPS = 64
LANES = 128
SETS = 16
BLOCKS = 128
SMEM = pl.BlockSpec(memory_space=pltpu.SMEM)
VMEM = pl.BlockSpec(memory_space=pltpu.VMEM)


def take(tile, index):
    return jnp.take_along_axis(tile, index, axis=1, mode="promise_in_bounds")


def list_offsets(counts_ref):
    offsets = [jnp.int32(0)]
    for i in range(LISTS):
        offsets.append(offsets[-1] + counts_ref[i])
    return offsets[:LISTS], offsets[LISTS]


def at_list(offsets, wanted):
    start = jnp.int32(0)
    for i in range(LISTS):
        start = jnp.where(wanted == i, offsets[i], start)
    return start


def group_size(live):
    return lax.shift_right_logical(live + (GROUPS - 1), 6)


def two_sizes(live):
    size = group_size(live)
    shift = jnp.minimum(lax.shift_right_logical(size * SHIFT, 5), jnp.maximum(LANES - size, 0))
    return size - shift, size + shift


def split_position(position, sizes):
    second = position >= 32 * sizes[0]
    rest = jnp.where(second, position - 32 * sizes[0], position)
    size = jnp.where(second, sizes[1], sizes[0])
    group = jnp.floor((rest.astype(F32) + 0.5) / size.astype(F32)).astype(I32)
    lane = rest - group * size
    group = jnp.where(second, group + 32, group)
    return group * 2 + (lane >> 7), lane & 127


def group_at(position, sizes):
    second = position >= 32 * sizes[0]
    rest = jnp.where(second, position - 32 * sizes[0], position)
    return lax.div(rest, jnp.where(second, sizes[1], sizes[0])) + jnp.where(second, 32, 0)


def pack_kernel(state_ref, mass_ref, elapsed_ref, ids_ref, out_ref):
    eighth = lax.axis_index("x") * 2 + lax.axis_index("c")
    part = pl.ds(pl.multiple_of(eighth * 256, 256), 256)
    piece = pl.ds(pl.multiple_of(lax.axis_index("z") * 256, 256), 256)
    old = state_ref[:, part]
    step = elapsed_ref[:, part]
    half = step * step * 0.5
    sixth = half * step / 3.0
    pos = old[0:3] + old[3:6] * step + old[6:9] * half + old[9:12] * sixth
    vel = old[3:6] + old[6:9] * step + old[9:12] * half
    mass = mass_ref[:, part] * (1.0 / 65536.0)
    ids = ids_ref[:, piece].astype(F32)
    rows = jnp.concatenate([pos, vel, mass, ids], axis=0)
    both = jnp.concatenate([rows[:, :LANES], rows[:, LANES:]], axis=0)
    for peer in range(32):
        out_ref[peer] = both


def extract_kernel(counts_ref, mine_ref, other_ref, out_ref):
    offsets, live = list_offsets(counts_ref)
    sizes = two_sizes(live)
    core = lax.axis_index("c")
    size = jnp.where(core == 0, sizes[0], sizes[1])
    begin = jnp.where(core == 0, 0, 32 * sizes[0]) + (lax.axis_index("z") * 4 + lax.axis_index("x")) * size
    my_y = lax.axis_index("y")
    halves = (mine_ref, other_ref)
    sub = lax.broadcasted_iota(I32, (8, LANES), 0)
    column = lax.broadcasted_iota(I32, (8, LANES), 1)

    def one_half(half):
        lane = column + half * LANES
        position = begin + lane
        valid = (lane < size) & (position < live)
        which = jnp.zeros((8, LANES), I32)
        base = jnp.zeros((8, LANES), I32)
        for i in range(1, LISTS):
            after = position >= offsets[i]
            which = jnp.where(after, i, which)
            base = jnp.where(after, offsets[i], base)
        slot = jnp.where(valid, position - base, 0)
        block = ((which & 1) ^ core) * 64 + (slot >> 8) * 8 + (which >> 1) * 2 + ((slot >> 7) & 1)
        within = slot & 127
        found = jnp.zeros((8, LANES), F32)
        for v in range(16):
            tile = halves[v >> 3][pl.ds(7 + 64 * (v & 7), 8, stride=8), :]
            found = jnp.where(block == v * 8 + sub, take(tile, within), found)
        star = jnp.broadcast_to(jnp.sum(found, axis=0, keepdims=True), (8, LANES)).astype(I32)
        mine = valid & ((star >> 14) == my_y)
        place = (((star >> 8) & 1) ^ core) * 64 + ((star >> 11) & 7) * 8 + ((star >> 9) & 3) * 2 + ((star >> 7) & 1)
        place = jnp.where(mine, place, -1)
        inside = star & 127
        picked = jnp.zeros((8, LANES), F32)
        for b in range(BLOCKS):
            tile = halves[b >> 6][(b & 63) * 8 : (b & 63) * 8 + 8, :]
            picked = jnp.where(place == b, take(tile, inside), picked)
        out_ref[half * 8 : half * 8 + 8, :] = jnp.where(sub < 6, picked, 0.0)

    one_half(0)
    out_ref[8:16, :] = jnp.zeros((8, LANES), F32)

    @pl.when(size > LANES)
    def _():
        one_half(1)


def plan_kernel(
    counts_ref, mine_ref, other_ref, state_ref, elapsed_ref,
    number_ref, first_ref, rank_ref, block_ref, lane_ref, slot_block_ref, slot_lane_ref, known_ref, one_ref, two_ref,
):
    offsets, live = list_offsets(counts_ref)
    sizes = two_sizes(live)
    shard = lax.axis_index("y") * 8 + lax.axis_index("z")
    wide = 2 * LANES
    row16 = lax.broadcasted_iota(I32, (16, wide), 0)
    row128 = lax.broadcasted_iota(I32, (LANES, wide), 0)
    column = lax.broadcasted_iota(I32, (1, wide), 1)
    square_row = lax.broadcasted_iota(I32, (LANES, LANES), 0)
    square_column = lax.broadcasted_iota(I32, (LANES, LANES), 1)
    contract = (((1,), (1,)), ((), ()))

    my_list = lax.axis_index("x") * 2 + lax.axis_index("c")
    start = at_list(offsets, my_list)
    slots = lax.broadcasted_iota(I32, (16, LANES), 0) * LANES + lax.broadcasted_iota(I32, (16, LANES), 1)
    block, lane = split_position(start + slots, sizes)
    slot_block_ref[...] = jnp.where(slots < counts_ref[my_list], block, -1)
    slot_lane_ref[...] = lane
    for b in range(CAP // LANES):
        first_ref[b] = group_at(start + b * LANES, sizes)
    first_ref[CAP // LANES] = lax.div(jnp.int32(LANES - 1), sizes[0]) + 2

    total = jnp.zeros((32, LANES), F32)
    for n in range(LISTS):
        i = (n & 6) + ((n & 1) ^ lax.axis_index("c"))
        count = counts_ref[i]
        start = at_list(offsets, i)
        half_ref = other_ref if n & 1 else mine_ref
        first = 7 + 8 * (n & 6)

        def step(turn, acc):
            even, odd = [
                half_ref[pl.ds(first + 8 * k + 256 * turn, 4, stride=64), :].astype(I32) for k in range(2)
            ]
            for k in range(0, 8, 2):
                ids = jnp.concatenate([even[k // 2 : k // 2 + 1], odd[k // 2 : k // 2 + 1]], axis=1)
                slot = turn * 1024 + k * LANES + column
                mine = (slot < count) & ((ids >> 11) == shard)
                high = jnp.where(mine, (ids >> 7) & 15, -1)
                low = ids & 127
                mark = start + slot + 1
                here = row16 == high
                left = jnp.concatenate(
                    [
                        jnp.where(here, (mark >> 7).astype(F32), 0.0),
                        jnp.where(here, (mark & 127).astype(F32), 0.0),
                    ],
                    axis=0,
                ).astype(jnp.bfloat16)
                right = jnp.where(row128 == low, 1.0, 0.0).astype(jnp.bfloat16)
                acc = acc + lax.dot_general(left, right, contract, preferred_element_type=F32)
            return acc

        total = lax.fori_loop(0, (count + 1023) >> 10, step, total)
    mark = (total[0:16] * 128.0 + total[16:32]).astype(I32)
    active = mark > 0
    flags = jnp.where(active, 1.0, 0.0).astype(jnp.bfloat16)
    upto = jnp.where(square_row <= square_column, 1.0, 0.0).astype(jnp.bfloat16)
    within = jnp.dot(flags, upto, preferred_element_type=F32)
    rows = jnp.broadcast_to(within[:, LANES - 1 :], (16, LANES)).astype(jnp.bfloat16)
    below = jnp.where(square_column[0:16, 0:16] < square_row[0:16, 0:16], 1.0, 0.0).astype(jnp.bfloat16)
    before = jnp.dot(below, rows, preferred_element_type=F32)
    rank = jnp.where(active, (within + before).astype(I32) - 1, -1)
    rank_ref[...] = rank
    number = jnp.sum(jnp.where(active, 1, 0))
    number_ref[0] = number
    row8 = lax.broadcasted_iota(I32, (8, LANES), 0)
    column8 = lax.broadcasted_iota(I32, (8, LANES), 1)

    def compact(turn, carry):
        sums = jnp.zeros((8, LANES), F32)
        for r in range(16):
            hit = jnp.where(rank[r : r + 1] - turn * LANES == square_row, 1.0, 0.0).astype(jnp.bfloat16)
            mine = mark[r : r + 1]
            facts = jnp.where(row8 == 0, mine >> 7, jnp.where(row8 == 1, mine & 127, jnp.where(row8 == 2, r, column8)))
            sums = sums + lax.dot_general(
                facts.astype(F32).astype(jnp.bfloat16), hit, contract, preferred_element_type=F32
            )
        mark_of = (sums[0:1] * 128.0 + sums[1:2]).astype(I32)
        block, lane = split_position(mark_of - 1, sizes)
        block_ref[pl.ds(turn, 1), :] = jnp.where(mark_of > 0, block, -1)
        lane_ref[pl.ds(turn, 1), :] = jnp.where(mark_of > 0, lane, 0)
        star_row = jnp.broadcast_to(sums[2:3], (8, LANES)).astype(I32)
        star_lane = jnp.broadcast_to(sums[3:4], (8, LANES)).astype(I32)
        head = jnp.zeros((8, LANES), F32)
        tail = jnp.zeros((8, LANES), F32)
        for r in range(16):
            part = slice(r * LANES, (r + 1) * LANES)
            here = star_row == r
            head = jnp.where(here, take(state_ref[0:8, part], star_lane), head)
            rest = jnp.concatenate(
                [state_ref[8:12, part], jnp.broadcast_to(elapsed_ref[:, part], (4, LANES))], axis=0
            )
            tail = jnp.where(here, take(rest, star_lane), tail)
        pos, vel = head[0:3], head[3:6]
        accel = jnp.concatenate([head[6:8], tail[0:1]], axis=0)
        jerk = tail[1:4]
        step_time = tail[4:5]
        half = step_time * 0.5
        twelfth = step_time * step_time / 12.0
        known_vel = vel + accel * half + jerk * twelfth
        known_pos = pos + (vel + known_vel) * half + accel * twelfth
        none = jnp.zeros((2, LANES), F32)
        wide3 = lambda value: jnp.broadcast_to(value, (3, LANES))
        begin = pl.ds(pl.multiple_of(turn * 8, 8), 8)
        known_ref[begin, :] = jnp.concatenate([known_pos, known_vel, none], axis=0)
        one_ref[begin, :] = jnp.concatenate([wide3(half * half - twelfth), wide3(half), none], axis=0)
        two_ref[begin, :] = jnp.concatenate([wide3(twelfth * half), wide3(twelfth), none], axis=0)
        return carry

    lax.fori_loop(0, jnp.maximum(((number + 255) >> 8) * 2, 2), compact, 0)


def pair_kernel(
    counts_ref, own_ref, one_ref, two_ref, three_ref, mine_ref, other_ref, out_ref,
    splat_ref, source_ref, part_ref,
):
    _, live = list_offsets(counts_ref)
    size = jnp.where(lax.axis_index("c") == 0, *two_sizes(live))
    column = lax.broadcasted_iota(I32, (8, LANES), 1)
    zero = jnp.zeros((8, LANES), F32)
    halves = (mine_ref, other_ref)
    targets = own_ref[...] + one_ref[...] + two_ref[...] + three_ref[...]

    for v in range(SETS):
        for c in range(7):
            at = (c * SETS + v) * 8
            source_ref[at : at + 8, :] = halves[v >> 3][pl.ds((v & 7) * 64 + c, 8, stride=8), :]

    def one_half(half):
        mine = targets[half * 8 : half * 8 + 8]
        for t in range(LANES):
            values = take(mine, jnp.full((8, LANES), t, I32))
            for c in range(6):
                at = (t * 6 + c) * 8
                splat_ref[at : at + 8, :] = jnp.broadcast_to(values[c : c + 1], (8, LANES))

        def four_targets(turn, carry):
            first = turn * 4
            sums = [zero] * 24
            for v in range(SETS):
                sx, sy, sz, vx, vy, vz, mass = [
                    source_ref[(c * SETS + v) * 8 : (c * SETS + v) * 8 + 8, :] for c in range(7)
                ]
                for t in range(4):
                    tx, ty, tz, ux, uy, uz = [
                        splat_ref[pl.ds(pl.multiple_of(((first + t) * 6 + c) * 8, 8), 8), :]
                        for c in range(6)
                    ]
                    rx = sx - tx
                    ry = sy - ty
                    rz = sz - tz
                    wx = vx - ux
                    wy = vy - uy
                    wz = vz - uz
                    square = (rx * rx + softening_square) + ry * ry + rz * rz
                    dot = rx * wx + ry * wy + rz * wz
                    inverse = lax.rsqrt(square)
                    inverse2 = inverse * inverse
                    weight = (mass * inverse) * inverse2
                    radial = (3.0 * dot) * inverse2
                    terms = (
                        rx, ry, rz,
                        wx - radial * rx, wy - radial * ry, wz - radial * rz,
                    )
                    for c in range(6):
                        sums[t * 6 + c] = sums[t * 6 + c] + weight * terms[c]
            for t in range(4):
                for c in range(6):
                    part_ref[pl.ds(pl.multiple_of((c * LANES + first + t) * 8, 8), 8), :] = sums[t * 6 + c]
            return carry

        count = jnp.minimum(size - half * LANES, LANES)
        lax.fori_loop(0, (count + 3) >> 2, four_targets, 0)
        rows = []
        for o in range(16):
            row = zero
            for c in range(6):
                first = (c * LANES + o * 8) * 8
                total = part_ref[pl.ds(first, 8, stride=8), :]
                for k in range(1, 8):
                    total = total + part_ref[pl.ds(first + k, 8, stride=8), :]
                row = jnp.where(column == c, jnp.sum(total, axis=1, keepdims=True), row)
            rows.append(row)
        out_ref[half * 8 : half * 8 + 8, :] = jnp.concatenate(rows, axis=0).T[0:8]

    one_half(0)

    @pl.when(size <= LANES)
    def _():
        out_ref[8:16, :] = zero

    @pl.when(size > LANES)
    def _():
        one_half(1)


def combine_kernel(own_ref, one_ref, two_ref, three_ref, out_ref, rest_ref):
    force = own_ref[...] + one_ref[...] + two_ref[...] + three_ref[...]
    for peer in range(32):
        out_ref[peer] = force[0:8]
    rest_ref[...] = force[8:16]


def finish_kernel(
    half, number_ref, first_ref, rank_ref, block_ref, lane_ref, slot_block_ref, slot_lane_ref, known_ref, one_ref, two_ref,
    mine_ref, other_ref, state_ref, *refs,
):
    new_ref, active_ref = refs[-2:]
    core = lax.axis_index("c")
    zero = jnp.zeros((8, LANES), F32)

    def wide(row):
        return jnp.broadcast_to(row, (8, LANES))

    def group_of(block):
        return jnp.where((block & 1) == half, block >> 1, -1)

    wanted = [group_of(wide(slot_block_ref[b : b + 1, :])) for b in range(CAP // LANES)]
    lanes = [wide(slot_lane_ref[b : b + 1, :]) for b in range(CAP // LANES)]
    firsts = [first_ref[b] for b in range(CAP // LANES)]

    def span(turn, acc):
        acc = list(acc)
        for b in range(CAP // LANES):
            group = jnp.minimum(firsts[b] + turn, GROUPS - 1)
            rows = pl.ds(pl.multiple_of((group & 31) * 8, 8), 8)
            forces = jnp.where((group >> 5) == core, mine_ref[rows, :], other_ref[rows, :])
            acc[b] = jnp.where(wanted[b] == group, take(forces, lanes[b]), acc[b])
        return tuple(acc)

    found = (zero,) * (CAP // LANES)
    for turn in range(3):
        found = span(jnp.int32(turn), found)
    found = lax.fori_loop(3, first_ref[CAP // LANES], span, found)
    for b in range(CAP // LANES):
        part = slice(b * LANES, (b + 1) * LANES)
        if half == 0:
            active_ref[:, part] = found[b][0:6]
        else:
            active_ref[:, part] = jnp.where(wanted[b][0:6] >= 0, found[b][0:6], refs[0][:, part])

    new_ref[...] = state_ref[...]
    none = jnp.zeros((2, LANES), F32)

    def moved(turn):
        group = group_of(wide(block_ref[pl.ds(turn, 1), :]))
        lane = wide(lane_ref[pl.ds(turn, 1), :])
        seen = group ^ (core * 32)
        force = zero
        for g in range(GROUPS):
            half_ref = mine_ref if g < 32 else other_ref
            force = jnp.where(seen == g, take(half_ref[(g & 31) * 8 : (g & 31) * 8 + 8, :], lane), force)
        begin = pl.ds(pl.multiple_of(turn * 8, 8), 8)
        accel = jnp.concatenate([force[0:3], force[0:3], none], axis=0)
        jerk = jnp.concatenate([force[3:6], force[3:6], none], axis=0)
        place = known_ref[begin, :] + accel * one_ref[begin, :] - jerk * two_ref[begin, :]
        head = jnp.concatenate([place[0:6], force[0:2]], axis=0)
        flag = jnp.where(group[0:4] >= 0, 1.0, 0.0)
        return head, jnp.concatenate([force[2:6], flag], axis=0)

    def compact(turn, carry):
        tiles = [moved(turn * 2), moved(turn * 2 + 1)]
        for r in range(16):
            part = slice(r * LANES, (r + 1) * LANES)
            rank = wide(rank_ref[r : r + 1, :])
            place = rank & 127
            top, bottom = new_ref[0:8, part], new_ref[8:12, part]
            for k, (head, tail) in enumerate(tiles):
                got = take(tail, place)
                here = (rank >> 7) == turn * 2 + k
                if half == 1:
                    here = here & (wide(got[7:8]) > 0.5)
                top = jnp.where(here, take(head, place), top)
                bottom = jnp.where(here[0:4], got[0:4], bottom)
            new_ref[0:8, part] = top
            new_ref[8:12, part] = bottom
        return carry

    compact(jnp.int32(0), 0)
    lax.fori_loop(1, (number_ref[0] + 255) >> 8, compact, 0)


def exchange_y(part):
    return [lax.ppermute(part, "y", [(i, (i + k) % 4) for i in range(4)]) for k in range(1, 4)]


def in_vmem(*arrays):
    return [pltpu.with_memory_space_constraint(array, pltpu.VMEM) for array in arrays]


def spread(part, *done):
    part = lax.all_to_all(part, ("z", "x"), 0, 0).reshape(-1, LANES)
    part, *done = lax.optimization_barrier((part, *done))
    return in_vmem(part, lax.ppermute(part, "c", [(0, 1), (1, 0)])), done


def finish(half, plan, forces, state, *rest):
    return pl.pallas_call(
        functools.partial(finish_kernel, half),
        out_shape=[
            jax.ShapeDtypeStruct((12, SHARD), F32),
            jax.ShapeDtypeStruct((6, CAP), F32),
        ],
        in_specs=[SMEM] * 2 + [VMEM] * (11 + len(rest)),
        out_specs=[VMEM, VMEM],
        name="finish",
    )(*plan[:2], *in_vmem(*plan[2:]), *forces, *in_vmem(state, *rest))


def body(state, mass, elapsed, active_ids, active_count):
    mass = mass.reshape(1, SHARD)
    elapsed = elapsed.reshape(1, SHARD)
    ids = active_ids.reshape(1, CAP)
    packed = pl.pallas_call(
        pack_kernel,
        out_shape=pltpu.VMEM((32, 16, LANES), F32),
        in_specs=[VMEM] * 4,
        out_specs=VMEM,
        name="pack",
    )(state, mass, elapsed, ids)
    slab, _ = spread(packed)
    own = pl.pallas_call(
        extract_kernel,
        out_shape=pltpu.VMEM((16, LANES), F32),
        in_specs=[SMEM, VMEM, VMEM],
        out_specs=VMEM,
        name="extract",
    )(active_count, *slab)
    others = exchange_y(own)
    square = pltpu.VMEM((LANES, LANES), F32)
    plan = pl.pallas_call(
        plan_kernel,
        out_shape=[jax.ShapeDtypeStruct((1,), I32), jax.ShapeDtypeStruct((CAP // LANES + 1,), I32)]
        + [pltpu.VMEM((16, LANES), I32)] * 5
        + [square] * 3,
        in_specs=[SMEM] + [VMEM] * 4,
        out_specs=[SMEM] * 2 + [VMEM] * 8,
        name="plan",
    )(active_count, *slab, *in_vmem(state, elapsed))
    partial = pl.pallas_call(
        pair_kernel,
        out_shape=pltpu.VMEM((16, LANES), F32),
        in_specs=[SMEM] + [VMEM] * 6,
        out_specs=VMEM,
        scratch_shapes=[
            pltpu.VMEM((LANES * 6 * 8, LANES), F32),
            pltpu.VMEM((7 * SETS * 8, LANES), F32),
            pltpu.VMEM((6 * LANES * 8, LANES), F32),
        ],
        compiler_params=pltpu.CompilerParams(vmem_limit_bytes=24 * 2**20),
        name="pairs",
    )(active_count, *in_vmem(own, *others), *slab)
    combined, rest = pl.pallas_call(
        combine_kernel,
        out_shape=[pltpu.VMEM((32, 8, LANES), F32), jax.ShapeDtypeStruct((8, LANES), F32)],
        in_specs=[VMEM] * 4,
        out_specs=[VMEM] * 2,
        name="combine",
    )(*in_vmem(partial, *exchange_y(partial)))
    turns = (group_size(jnp.sum(active_count)) > LANES).astype(I32)
    forces, (turns, *plan) = spread(combined, turns, *plan)
    outputs = finish(0, plan, forces, state)

    def more(carry):
        turn, new_state, active_force = carry
        forces, _ = spread(jnp.broadcast_to(rest[None], (32, 8, LANES)))
        return (turn + 1, *finish(1, plan, forces, new_state, active_force))

    return lax.while_loop(lambda carry: carry[0] < turns, more, (jnp.int32(0), *outputs))[1:]


def solution(mesh):
    fine = Mesh(mesh.devices.reshape(4, 2, 4, 8), ("x", "c", "y", "z"))
    placed = (P(None, ("y", "z")), P(("y", "z")), P(("y", "z")), P(("x", "c")), P())
    return jax.shard_map(
        body,
        mesh=fine,
        in_specs=placed,
        out_specs=(P(None, ("y", "z")), P(None, ("x", "c"))),
        check_vma=False,
    )
```

```python
import functools

import jax
import jax.numpy as jnp
from jax import lax
from jax.experimental import pallas as pl
from jax.experimental.pallas import tpu as pltpu
from jax.sharding import Mesh, PartitionSpec as P

F32 = jnp.float32
I32 = jnp.int32
softening_square = 0.01
LISTS = 8
CAP = 2048
SHIFT = 5
SHARD = 2048
GROUPS = 64
LANES = 128
SETS = 16
BLOCKS = 128
SMEM = pl.BlockSpec(memory_space=pltpu.SMEM)
VMEM = pl.BlockSpec(memory_space=pltpu.VMEM)


def take(tile, index):
    return jnp.take_along_axis(tile, index, axis=1, mode="promise_in_bounds")


def list_offsets(counts_ref):
    offsets = [jnp.int32(0)]
    for i in range(LISTS):
        offsets.append(offsets[-1] + counts_ref[i])
    return offsets[:LISTS], offsets[LISTS]


def at_list(offsets, wanted):
    start = jnp.int32(0)
    for i in range(LISTS):
        start = jnp.where(wanted == i, offsets[i], start)
    return start


def group_size(live):
    return lax.shift_right_logical(live + (GROUPS - 1), 6)


def two_sizes(live):
    size = group_size(live)
    shift = jnp.minimum(lax.shift_right_logical(size * SHIFT, 5), jnp.maximum(LANES - size, 0))
    return size - shift, size + shift


def split_position(position, sizes):
    second = position >= 32 * sizes[0]
    rest = jnp.where(second, position - 32 * sizes[0], position)
    size = jnp.where(second, sizes[1], sizes[0])
    group = jnp.floor((rest.astype(F32) + 0.5) / size.astype(F32)).astype(I32)
    lane = rest - group * size
    group = jnp.where(second, group + 32, group)
    return group * 2 + (lane >> 7), lane & 127


def group_at(position, sizes):
    second = position >= 32 * sizes[0]
    rest = jnp.where(second, position - 32 * sizes[0], position)
    return lax.div(rest, jnp.where(second, sizes[1], sizes[0])) + jnp.where(second, 32, 0)


def pack_kernel(state_ref, mass_ref, elapsed_ref, ids_ref, out_ref):
    eighth = lax.axis_index("x") * 2 + lax.axis_index("c")
    part = pl.ds(pl.multiple_of(eighth * 256, 256), 256)
    piece = pl.ds(pl.multiple_of(lax.axis_index("z") * 256, 256), 256)
    old = state_ref[:, part]
    step = elapsed_ref[:, part]
    half = step * step * 0.5
    sixth = half * step / 3.0
    pos = old[0:3] + old[3:6] * step + old[6:9] * half + old[9:12] * sixth
    vel = old[3:6] + old[6:9] * step + old[9:12] * half
    mass = mass_ref[:, part] * (1.0 / 65536.0)
    ids = ids_ref[:, piece].astype(F32)
    rows = jnp.concatenate([pos, vel, mass, ids], axis=0)
    both = jnp.concatenate([rows[:, :LANES], rows[:, LANES:]], axis=0)
    for peer in range(32):
        out_ref[peer] = both


def extract_kernel(counts_ref, mine_ref, other_ref, out_ref):
    offsets, live = list_offsets(counts_ref)
    sizes = two_sizes(live)
    core = lax.axis_index("c")
    size = jnp.where(core == 0, sizes[0], sizes[1])
    begin = jnp.where(core == 0, 0, 32 * sizes[0]) + (lax.axis_index("z") * 4 + lax.axis_index("x")) * size
    my_y = lax.axis_index("y")
    halves = (mine_ref, other_ref)
    sub = lax.broadcasted_iota(I32, (8, LANES), 0)
    column = lax.broadcasted_iota(I32, (8, LANES), 1)

    def one_half(half):
        lane = column + half * LANES
        position = begin + lane
        valid = (lane < size) & (position < live)
        which = jnp.zeros((8, LANES), I32)
        base = jnp.zeros((8, LANES), I32)
        for i in range(1, LISTS):
            after = position >= offsets[i]
            which = jnp.where(after, i, which)
            base = jnp.where(after, offsets[i], base)
        slot = jnp.where(valid, position - base, 0)
        block = ((which & 1) ^ core) * 64 + (slot >> 8) * 8 + (which >> 1) * 2 + ((slot >> 7) & 1)
        within = slot & 127
        found = jnp.zeros((8, LANES), F32)
        for v in range(16):
            tile = halves[v >> 3][pl.ds(7 + 64 * (v & 7), 8, stride=8), :]
            found = jnp.where(block == v * 8 + sub, take(tile, within), found)
        star = jnp.broadcast_to(jnp.sum(found, axis=0, keepdims=True), (8, LANES)).astype(I32)
        mine = valid & ((star >> 14) == my_y)
        place = (((star >> 8) & 1) ^ core) * 64 + ((star >> 11) & 7) * 8 + ((star >> 9) & 3) * 2 + ((star >> 7) & 1)
        place = jnp.where(mine, place, -1)
        inside = star & 127
        picked = jnp.zeros((8, LANES), F32)
        for b in range(BLOCKS):
            tile = halves[b >> 6][(b & 63) * 8 : (b & 63) * 8 + 8, :]
            picked = jnp.where(place == b, take(tile, inside), picked)
        out_ref[half * 8 : half * 8 + 8, :] = jnp.where(sub < 6, picked, 0.0)

    one_half(0)
    out_ref[8:16, :] = jnp.zeros((8, LANES), F32)

    @pl.when(size > LANES)
    def _():
        one_half(1)


def plan_kernel(
    counts_ref, mine_ref, other_ref, state_ref, elapsed_ref,
    number_ref, first_ref, rank_ref, block_ref, lane_ref, slot_block_ref, slot_lane_ref, known_ref, one_ref, two_ref,
):
    offsets, live = list_offsets(counts_ref)
    sizes = two_sizes(live)
    shard = lax.axis_index("y") * 8 + lax.axis_index("z")
    wide = 2 * LANES
    row16 = lax.broadcasted_iota(I32, (16, wide), 0)
    row128 = lax.broadcasted_iota(I32, (LANES, wide), 0)
    column = lax.broadcasted_iota(I32, (1, wide), 1)
    square_row = lax.broadcasted_iota(I32, (LANES, LANES), 0)
    square_column = lax.broadcasted_iota(I32, (LANES, LANES), 1)
    contract = (((1,), (1,)), ((), ()))

    my_list = lax.axis_index("x") * 2 + lax.axis_index("c")
    start = at_list(offsets, my_list)
    slots = lax.broadcasted_iota(I32, (16, LANES), 0) * LANES + lax.broadcasted_iota(I32, (16, LANES), 1)
    block, lane = split_position(start + slots, sizes)
    slot_block_ref[...] = jnp.where(slots < counts_ref[my_list], block, -1)
    slot_lane_ref[...] = lane
    for b in range(CAP // LANES):
        first_ref[b] = group_at(start + b * LANES, sizes)
    first_ref[CAP // LANES] = lax.div(jnp.int32(LANES - 1), sizes[0]) + 2

    total = jnp.zeros((32, LANES), F32)
    for n in range(LISTS):
        i = (n & 6) + ((n & 1) ^ lax.axis_index("c"))
        count = counts_ref[i]
        start = at_list(offsets, i)
        half_ref = other_ref if n & 1 else mine_ref
        first = 7 + 8 * (n & 6)

        def step(turn, acc):
            even, odd = [
                half_ref[pl.ds(first + 8 * k + 256 * turn, 4, stride=64), :].astype(I32) for k in range(2)
            ]
            for k in range(0, 8, 2):
                ids = jnp.concatenate([even[k // 2 : k // 2 + 1], odd[k // 2 : k // 2 + 1]], axis=1)
                slot = turn * 1024 + k * LANES + column
                mine = (slot < count) & ((ids >> 11) == shard)
                high = jnp.where(mine, (ids >> 7) & 15, -1)
                low = ids & 127
                mark = start + slot + 1
                here = row16 == high
                left = jnp.concatenate(
                    [
                        jnp.where(here, (mark >> 7).astype(F32), 0.0),
                        jnp.where(here, (mark & 127).astype(F32), 0.0),
                    ],
                    axis=0,
                ).astype(jnp.bfloat16)
                right = jnp.where(row128 == low, 1.0, 0.0).astype(jnp.bfloat16)
                acc = acc + lax.dot_general(left, right, contract, preferred_element_type=F32)
            return acc

        total = lax.fori_loop(0, (count + 1023) >> 10, step, total)
    mark = (total[0:16] * 128.0 + total[16:32]).astype(I32)
    active = mark > 0
    flags = jnp.where(active, 1.0, 0.0).astype(jnp.bfloat16)
    upto = jnp.where(square_row <= square_column, 1.0, 0.0).astype(jnp.bfloat16)
    within = jnp.dot(flags, upto, preferred_element_type=F32)
    rows = jnp.broadcast_to(within[:, LANES - 1 :], (16, LANES)).astype(jnp.bfloat16)
    below = jnp.where(square_column[0:16, 0:16] < square_row[0:16, 0:16], 1.0, 0.0).astype(jnp.bfloat16)
    before = jnp.dot(below, rows, preferred_element_type=F32)
    rank = jnp.where(active, (within + before).astype(I32) - 1, -1)
    rank_ref[...] = rank
    number = jnp.sum(jnp.where(active, 1, 0))
    number_ref[0] = number
    row8 = lax.broadcasted_iota(I32, (8, LANES), 0)
    column8 = lax.broadcasted_iota(I32, (8, LANES), 1)

    def compact(turn, carry):
        sums = jnp.zeros((8, LANES), F32)
        for r in range(16):
            hit = jnp.where(rank[r : r + 1] - turn * LANES == square_row, 1.0, 0.0).astype(jnp.bfloat16)
            mine = mark[r : r + 1]
            facts = jnp.where(row8 == 0, mine >> 7, jnp.where(row8 == 1, mine & 127, jnp.where(row8 == 2, r, column8)))
            sums = sums + lax.dot_general(
                facts.astype(F32).astype(jnp.bfloat16), hit, contract, preferred_element_type=F32
            )
        mark_of = (sums[0:1] * 128.0 + sums[1:2]).astype(I32)
        block, lane = split_position(mark_of - 1, sizes)
        block_ref[pl.ds(turn, 1), :] = jnp.where(mark_of > 0, block, -1)
        lane_ref[pl.ds(turn, 1), :] = jnp.where(mark_of > 0, lane, 0)
        star_row = jnp.broadcast_to(sums[2:3], (8, LANES)).astype(I32)
        star_lane = jnp.broadcast_to(sums[3:4], (8, LANES)).astype(I32)
        head = jnp.zeros((8, LANES), F32)
        tail = jnp.zeros((8, LANES), F32)
        for r in range(16):
            part = slice(r * LANES, (r + 1) * LANES)
            here = star_row == r
            head = jnp.where(here, take(state_ref[0:8, part], star_lane), head)
            rest = jnp.concatenate(
                [state_ref[8:12, part], jnp.broadcast_to(elapsed_ref[:, part], (4, LANES))], axis=0
            )
            tail = jnp.where(here, take(rest, star_lane), tail)
        pos, vel = head[0:3], head[3:6]
        accel = jnp.concatenate([head[6:8], tail[0:1]], axis=0)
        jerk = tail[1:4]
        step_time = tail[4:5]
        half = step_time * 0.5
        twelfth = step_time * step_time / 12.0
        known_vel = vel + accel * half + jerk * twelfth
        known_pos = pos + (vel + known_vel) * half + accel * twelfth
        none = jnp.zeros((2, LANES), F32)
        wide3 = lambda value: jnp.broadcast_to(value, (3, LANES))
        begin = pl.ds(pl.multiple_of(turn * 8, 8), 8)
        known_ref[begin, :] = jnp.concatenate([known_pos, known_vel, none], axis=0)
        one_ref[begin, :] = jnp.concatenate([wide3(half * half - twelfth), wide3(half), none], axis=0)
        two_ref[begin, :] = jnp.concatenate([wide3(twelfth * half), wide3(twelfth), none], axis=0)
        return carry

    lax.fori_loop(0, jnp.maximum(((number + 255) >> 8) * 2, 2), compact, 0)


def pair_kernel(
    counts_ref, own_ref, one_ref, two_ref, three_ref, mine_ref, other_ref, out_ref,
    splat_ref, source_ref, part_ref, sum_ref,
):
    _, live = list_offsets(counts_ref)
    size = jnp.where(lax.axis_index("c") == 0, *two_sizes(live))
    column = lax.broadcasted_iota(I32, (8, LANES), 1)
    zero = jnp.zeros((8, LANES), F32)
    halves = (mine_ref, other_ref)
    targets = own_ref[...] + one_ref[...] + two_ref[...] + three_ref[...]

    for v in range(SETS):
        for c in range(7):
            at = (c * SETS + v) * 8
            source_ref[at : at + 8, :] = halves[v >> 3][pl.ds((v & 7) * 64 + c, 8, stride=8), :]

    def one_half(half):
        mine = targets[half * 8 : half * 8 + 8]
        count = jnp.minimum(size - half * LANES, LANES)

        def splat(chunk):
            for t in range(chunk * 32, chunk * 32 + 32):
                values = take(mine, jnp.full((8, LANES), t, I32))
                for c in range(6):
                    at = (t * 6 + c) * 8
                    splat_ref[at : at + 8, :] = jnp.broadcast_to(values[c : c + 1], (8, LANES))

        splat(0)
        for chunk in range(1, 4):
            pl.when(count > chunk * 32)(functools.partial(splat, chunk))

        def four_targets(turn, carry):
            first = turn * 4
            sums = [zero] * 36
            for v in range(SETS):
                sx, sy, sz, vx, vy, vz, mass = [
                    source_ref[(c * SETS + v) * 8 : (c * SETS + v) * 8 + 8, :] for c in range(7)
                ]
                for t in range(4):
                    tx, ty, tz, ux, uy, uz = [
                        splat_ref[pl.ds(pl.multiple_of(((first + t) * 6 + c) * 8, 8), 8), :]
                        for c in range(6)
                    ]
                    rx = sx - tx
                    ry = sy - ty
                    rz = sz - tz
                    wx = vx - ux
                    wy = vy - uy
                    wz = vz - uz
                    square = (rx * rx + softening_square) + ry * ry + rz * rz
                    dot = rx * wx + ry * wy + rz * wz
                    inverse = lax.rsqrt(square)
                    inverse2 = inverse * inverse
                    weight = (mass * inverse) * inverse2
                    radial = dot * inverse2
                    pulls = (weight * rx, weight * ry, weight * rz)
                    drifts = (weight * wx, weight * wy, weight * wz)
                    for c in range(3):
                        sums[t * 9 + c] = sums[t * 9 + c] + pulls[c]
                        sums[t * 9 + 3 + c] = sums[t * 9 + 3 + c] + drifts[c]
                        sums[t * 9 + 6 + c] = sums[t * 9 + 6 + c] + radial * pulls[c]
            for t in range(4):
                for c in range(6):
                    total = sums[t * 9 + c]
                    if c >= 3:
                        total = total - 3.0 * sums[t * 9 + 3 + c]
                    part_ref[pl.ds(pl.multiple_of((c * LANES + first + t) * 8, 8), 8), :] = total
            return carry

        lax.fori_loop(0, (count + 3) >> 2, four_targets, 0)

        def gather_sums(octets):
            for o in octets:
                one_octet(o)

        def one_octet(o):
            row = zero
            for c in range(6):
                first = (c * LANES + o * 8) * 8
                total = part_ref[pl.ds(first, 8, stride=8), :]
                for k in range(1, 8):
                    total = total + part_ref[pl.ds(first + k, 8, stride=8), :]
                row = jnp.where(column == c, jnp.sum(total, axis=1, keepdims=True), row)
            sum_ref[o * 8 : o * 8 + 8, :] = row

        gather_sums(range(4))
        for chunk in range(1, 4):
            pl.when(count > chunk * 32)(functools.partial(gather_sums, range(chunk * 4, chunk * 4 + 4)))
        out_ref[half * 8 : half * 8 + 8, :] = sum_ref[...].T[0:8]

    one_half(0)

    @pl.when(size <= LANES)
    def _():
        out_ref[8:16, :] = zero

    @pl.when(size > LANES)
    def _():
        one_half(1)


def combine_kernel(own_ref, one_ref, two_ref, three_ref, out_ref, rest_ref):
    force = own_ref[...] + one_ref[...] + two_ref[...] + three_ref[...]
    for peer in range(32):
        out_ref[peer] = force[0:8]
    rest_ref[...] = force[8:16]


def finish_kernel(
    half, number_ref, first_ref, rank_ref, block_ref, lane_ref, slot_block_ref, slot_lane_ref, known_ref, one_ref, two_ref,
    mine_ref, other_ref, state_ref, *refs,
):
    new_ref, active_ref = refs[-2:]
    core = lax.axis_index("c")
    zero = jnp.zeros((8, LANES), F32)

    def wide(row):
        return jnp.broadcast_to(row, (8, LANES))

    def group_of(block):
        return jnp.where((block & 1) == half, block >> 1, -1)

    wanted = [group_of(wide(slot_block_ref[b : b + 1, :])) for b in range(CAP // LANES)]
    lanes = [wide(slot_lane_ref[b : b + 1, :]) for b in range(CAP // LANES)]
    firsts = [first_ref[b] for b in range(CAP // LANES)]

    def span(turn, acc):
        acc = list(acc)
        for b in range(CAP // LANES):
            group = jnp.minimum(firsts[b] + turn, GROUPS - 1)
            rows = pl.ds(pl.multiple_of((group & 31) * 8, 8), 8)
            forces = jnp.where((group >> 5) == core, mine_ref[rows, :], other_ref[rows, :])
            acc[b] = jnp.where(wanted[b] == group, take(forces, lanes[b]), acc[b])
        return tuple(acc)

    found = (zero,) * (CAP // LANES)
    for turn in range(3):
        found = span(jnp.int32(turn), found)
    found = lax.fori_loop(3, first_ref[CAP // LANES], span, found)
    for b in range(CAP // LANES):
        part = slice(b * LANES, (b + 1) * LANES)
        if half == 0:
            active_ref[:, part] = found[b][0:6]
        else:
            active_ref[:, part] = jnp.where(wanted[b][0:6] >= 0, found[b][0:6], refs[0][:, part])

    new_ref[...] = state_ref[...]
    none = jnp.zeros((2, LANES), F32)

    def moved(turn):
        group = group_of(wide(block_ref[pl.ds(turn, 1), :]))
        lane = wide(lane_ref[pl.ds(turn, 1), :])
        seen = group ^ (core * 32)
        force = zero
        for g in range(GROUPS):
            half_ref = mine_ref if g < 32 else other_ref
            force = jnp.where(seen == g, take(half_ref[(g & 31) * 8 : (g & 31) * 8 + 8, :], lane), force)
        begin = pl.ds(pl.multiple_of(turn * 8, 8), 8)
        accel = jnp.concatenate([force[0:3], force[0:3], none], axis=0)
        jerk = jnp.concatenate([force[3:6], force[3:6], none], axis=0)
        place = known_ref[begin, :] + accel * one_ref[begin, :] - jerk * two_ref[begin, :]
        head = jnp.concatenate([place[0:6], force[0:2]], axis=0)
        flag = jnp.where(group[0:4] >= 0, 1.0, 0.0)
        return head, jnp.concatenate([force[2:6], flag], axis=0)

    def compact(turn, carry):
        tiles = [moved(turn * 2), moved(turn * 2 + 1)]
        for r in range(16):
            part = slice(r * LANES, (r + 1) * LANES)
            rank = wide(rank_ref[r : r + 1, :])
            place = rank & 127
            top, bottom = new_ref[0:8, part], new_ref[8:12, part]
            for k, (head, tail) in enumerate(tiles):
                got = take(tail, place)
                here = (rank >> 7) == turn * 2 + k
                if half == 1:
                    here = here & (wide(got[7:8]) > 0.5)
                top = jnp.where(here, take(head, place), top)
                bottom = jnp.where(here[0:4], got[0:4], bottom)
            new_ref[0:8, part] = top
            new_ref[8:12, part] = bottom
        return carry

    compact(jnp.int32(0), 0)
    lax.fori_loop(1, (number_ref[0] + 255) >> 8, compact, 0)


def exchange_y(part):
    return [lax.ppermute(part, "y", [(i, (i + k) % 4) for i in range(4)]) for k in range(1, 4)]


def in_vmem(*arrays):
    return [pltpu.with_memory_space_constraint(array, pltpu.VMEM) for array in arrays]


def spread(part, *done):
    part = lax.all_to_all(part, ("z", "x"), 0, 0).reshape(-1, LANES)
    part, *done = lax.optimization_barrier((part, *done))
    return in_vmem(part, lax.ppermute(part, "c", [(0, 1), (1, 0)])), done


def finish(half, plan, forces, state, *rest):
    return pl.pallas_call(
        functools.partial(finish_kernel, half),
        out_shape=[
            jax.ShapeDtypeStruct((12, SHARD), F32),
            jax.ShapeDtypeStruct((6, CAP), F32),
        ],
        in_specs=[SMEM] * 2 + [VMEM] * (11 + len(rest)),
        out_specs=[VMEM, VMEM],
        name="finish",
    )(*plan[:2], *in_vmem(*plan[2:]), *forces, *in_vmem(state, *rest))


def body(state, mass, elapsed, active_ids, active_count):
    mass = mass.reshape(1, SHARD)
    elapsed = elapsed.reshape(1, SHARD)
    ids = active_ids.reshape(1, CAP)
    packed = pl.pallas_call(
        pack_kernel,
        out_shape=pltpu.VMEM((32, 16, LANES), F32),
        in_specs=[VMEM] * 4,
        out_specs=VMEM,
        name="pack",
    )(state, mass, elapsed, ids)
    slab, _ = spread(packed)
    own = pl.pallas_call(
        extract_kernel,
        out_shape=pltpu.VMEM((16, LANES), F32),
        in_specs=[SMEM, VMEM, VMEM],
        out_specs=VMEM,
        name="extract",
    )(active_count, *slab)
    others = exchange_y(own)
    square = pltpu.VMEM((LANES, LANES), F32)
    plan = pl.pallas_call(
        plan_kernel,
        out_shape=[jax.ShapeDtypeStruct((1,), I32), jax.ShapeDtypeStruct((CAP // LANES + 1,), I32)]
        + [pltpu.VMEM((16, LANES), I32)] * 5
        + [square] * 3,
        in_specs=[SMEM] + [VMEM] * 4,
        out_specs=[SMEM] * 2 + [VMEM] * 8,
        name="plan",
    )(active_count, *slab, *in_vmem(state, elapsed))
    partial = pl.pallas_call(
        pair_kernel,
        out_shape=pltpu.VMEM((16, LANES), F32),
        in_specs=[SMEM] + [VMEM] * 6,
        out_specs=VMEM,
        scratch_shapes=[
            pltpu.VMEM((LANES * 6 * 8, LANES), F32),
            pltpu.VMEM((7 * SETS * 8, LANES), F32),
            pltpu.VMEM((6 * LANES * 8, LANES), F32),
            pltpu.VMEM((LANES, LANES), F32),
        ],
        compiler_params=pltpu.CompilerParams(vmem_limit_bytes=24 * 2**20),
        name="pairs",
    )(active_count, *in_vmem(own, *others), *slab)
    combined, rest = pl.pallas_call(
        combine_kernel,
        out_shape=[pltpu.VMEM((32, 8, LANES), F32), pltpu.VMEM((8, LANES), F32)],
        in_specs=[VMEM] * 4,
        out_specs=[VMEM] * 2,
        name="combine",
    )(*in_vmem(partial, *exchange_y(partial)))
    turns = (group_size(jnp.sum(active_count)) > LANES).astype(I32)
    forces, (turns, *plan) = spread(combined, turns, *plan)
    outputs = finish(0, plan, forces, state)

    def more(carry):
        turn, new_state, active_force = carry
        forces, _ = spread(jnp.broadcast_to(rest[None], (32, 8, LANES)))
        return (turn + 1, *finish(1, plan, forces, new_state, active_force))

    return lax.while_loop(lambda carry: carry[0] < turns, more, (jnp.int32(0), *outputs))[1:]


def solution(mesh):
    fine = Mesh(mesh.devices.reshape(4, 2, 4, 8), ("x", "c", "y", "z"))
    placed = (P(None, ("y", "z")), P(("y", "z")), P(("y", "z")), P(("x", "c")), P())
    return jax.shard_map(
        body,
        mesh=fine,
        in_specs=placed,
        out_specs=(P(None, ("y", "z")), P(None, ("x", "c"))),
        check_vma=False,
    )
```

```python
import functools

import jax
import jax.numpy as jnp
from jax import lax
from jax.experimental import pallas as pl
from jax.experimental.pallas import tpu as pltpu
from jax.sharding import Mesh, PartitionSpec as P

F32 = jnp.float32
I32 = jnp.int32
softening_square = 0.01
LISTS = 8
CAP = 2048
SHIFT = 6
SHARD = 2048
GROUPS = 64
LANES = 128
SETS = 16
BLOCKS = 128
SMEM = pl.BlockSpec(memory_space=pltpu.SMEM)
VMEM = pl.BlockSpec(memory_space=pltpu.VMEM)


def take(tile, index):
    return jnp.take_along_axis(tile, index, axis=1, mode="promise_in_bounds")


def list_offsets(counts_ref):
    offsets = [jnp.int32(0)]
    for i in range(LISTS):
        offsets.append(offsets[-1] + counts_ref[i])
    return offsets[:LISTS], offsets[LISTS]


def at_list(offsets, wanted):
    start = jnp.int32(0)
    for i in range(LISTS):
        start = jnp.where(wanted == i, offsets[i], start)
    return start


def group_size(live):
    return lax.shift_right_logical(live + (GROUPS - 1), 6)


def two_sizes(live):
    size = group_size(live)
    shift = jnp.minimum(lax.shift_right_logical(size * SHIFT, 5), jnp.maximum(LANES - size, 0))
    return size - shift, size + shift


def split_position(position, sizes):
    second = position >= 32 * sizes[0]
    rest = jnp.where(second, position - 32 * sizes[0], position)
    size = jnp.where(second, sizes[1], sizes[0])
    group = jnp.floor((rest.astype(F32) + 0.5) / size.astype(F32)).astype(I32)
    lane = rest - group * size
    group = jnp.where(second, group + 32, group)
    return group * 2 + (lane >> 7), lane & 127


def group_at(position, sizes):
    second = position >= 32 * sizes[0]
    rest = jnp.where(second, position - 32 * sizes[0], position)
    return lax.div(rest, jnp.where(second, sizes[1], sizes[0])) + jnp.where(second, 32, 0)


def pack_kernel(state_ref, mass_ref, elapsed_ref, ids_ref, out_ref):
    eighth = lax.axis_index("x") * 2 + lax.axis_index("c")
    part = pl.ds(pl.multiple_of(eighth * 256, 256), 256)
    piece = pl.ds(pl.multiple_of(lax.axis_index("z") * 256, 256), 256)
    old = state_ref[:, part]
    step = elapsed_ref[:, part]
    half = step * step * 0.5
    sixth = half * step / 3.0
    pos = old[0:3] + old[3:6] * step + old[6:9] * half + old[9:12] * sixth
    vel = old[3:6] + old[6:9] * step + old[9:12] * half
    mass = mass_ref[:, part] * (1.0 / 65536.0)
    ids = ids_ref[:, piece].astype(F32)
    rows = jnp.concatenate([pos, vel, mass, ids], axis=0)
    both = jnp.concatenate([rows[:, :LANES], rows[:, LANES:]], axis=0)
    for peer in range(32):
        out_ref[peer] = both


def extract_kernel(counts_ref, mine_ref, other_ref, out_ref):
    offsets, live = list_offsets(counts_ref)
    sizes = two_sizes(live)
    core = lax.axis_index("c")
    size = jnp.where(core == 0, sizes[0], sizes[1])
    begin = jnp.where(core == 0, 0, 32 * sizes[0]) + (lax.axis_index("z") * 4 + lax.axis_index("x")) * size
    my_y = lax.axis_index("y")
    halves = (mine_ref, other_ref)
    sub = lax.broadcasted_iota(I32, (8, LANES), 0)
    column = lax.broadcasted_iota(I32, (8, LANES), 1)

    def one_half(half):
        lane = column + half * LANES
        position = begin + lane
        valid = (lane < size) & (position < live)
        which = jnp.zeros((8, LANES), I32)
        base = jnp.zeros((8, LANES), I32)
        for i in range(1, LISTS):
            after = position >= offsets[i]
            which = jnp.where(after, i, which)
            base = jnp.where(after, offsets[i], base)
        slot = jnp.where(valid, position - base, 0)
        block = ((which & 1) ^ core) * 64 + (slot >> 8) * 8 + (which >> 1) * 2 + ((slot >> 7) & 1)
        within = slot & 127
        found = jnp.zeros((8, LANES), F32)
        for v in range(16):
            tile = halves[v >> 3][pl.ds(7 + 64 * (v & 7), 8, stride=8), :]
            found = jnp.where(block == v * 8 + sub, take(tile, within), found)
        star = jnp.broadcast_to(jnp.sum(found, axis=0, keepdims=True), (8, LANES)).astype(I32)
        mine = valid & ((star >> 14) == my_y)
        place = (((star >> 8) & 1) ^ core) * 64 + ((star >> 11) & 7) * 8 + ((star >> 9) & 3) * 2 + ((star >> 7) & 1)
        place = jnp.where(mine, place, -1)
        inside = star & 127
        picked = jnp.zeros((8, LANES), F32)
        for b in range(BLOCKS):
            tile = halves[b >> 6][(b & 63) * 8 : (b & 63) * 8 + 8, :]
            picked = jnp.where(place == b, take(tile, inside), picked)
        out_ref[half * 8 : half * 8 + 8, :] = jnp.where(sub < 6, picked, 0.0)

    one_half(0)
    out_ref[8:16, :] = jnp.zeros((8, LANES), F32)

    @pl.when(size > LANES)
    def _():
        one_half(1)


def plan_kernel(
    counts_ref, mine_ref, other_ref, state_ref, elapsed_ref,
    number_ref, first_ref, rank_ref, block_ref, lane_ref, slot_block_ref, slot_lane_ref, known_ref, one_ref, two_ref,
):
    offsets, live = list_offsets(counts_ref)
    sizes = two_sizes(live)
    shard = lax.axis_index("y") * 8 + lax.axis_index("z")
    wide = 2 * LANES
    row16 = lax.broadcasted_iota(I32, (16, wide), 0)
    row128 = lax.broadcasted_iota(I32, (LANES, wide), 0)
    column = lax.broadcasted_iota(I32, (1, wide), 1)
    square_row = lax.broadcasted_iota(I32, (LANES, LANES), 0)
    square_column = lax.broadcasted_iota(I32, (LANES, LANES), 1)
    contract = (((1,), (1,)), ((), ()))

    my_list = lax.axis_index("x") * 2 + lax.axis_index("c")
    start = at_list(offsets, my_list)
    slots = lax.broadcasted_iota(I32, (16, LANES), 0) * LANES + lax.broadcasted_iota(I32, (16, LANES), 1)
    block, lane = split_position(start + slots, sizes)
    slot_block_ref[...] = jnp.where(slots < counts_ref[my_list], block, -1)
    slot_lane_ref[...] = lane
    for b in range(CAP // LANES):
        first_ref[b] = group_at(start + b * LANES, sizes)
    first_ref[CAP // LANES] = lax.div(jnp.int32(LANES - 1), sizes[0]) + 2

    total = jnp.zeros((32, LANES), F32)
    for n in range(LISTS):
        i = (n & 6) + ((n & 1) ^ lax.axis_index("c"))
        count = counts_ref[i]
        start = at_list(offsets, i)
        half_ref = other_ref if n & 1 else mine_ref
        first = 7 + 8 * (n & 6)

        def step(turn, acc):
            even, odd = [
                half_ref[pl.ds(first + 8 * k + 256 * turn, 4, stride=64), :].astype(I32) for k in range(2)
            ]
            for k in range(0, 8, 2):
                ids = jnp.concatenate([even[k // 2 : k // 2 + 1], odd[k // 2 : k // 2 + 1]], axis=1)
                slot = turn * 1024 + k * LANES + column
                mine = (slot < count) & ((ids >> 11) == shard)
                high = jnp.where(mine, (ids >> 7) & 15, -1)
                low = ids & 127
                mark = start + slot + 1
                here = row16 == high
                left = jnp.concatenate(
                    [
                        jnp.where(here, (mark >> 7).astype(F32), 0.0),
                        jnp.where(here, (mark & 127).astype(F32), 0.0),
                    ],
                    axis=0,
                ).astype(jnp.bfloat16)
                right = jnp.where(row128 == low, 1.0, 0.0).astype(jnp.bfloat16)
                acc = acc + lax.dot_general(left, right, contract, preferred_element_type=F32)
            return acc

        total = lax.fori_loop(0, (count + 1023) >> 10, step, total)
    mark = (total[0:16] * 128.0 + total[16:32]).astype(I32)
    active = mark > 0
    flags = jnp.where(active, 1.0, 0.0).astype(jnp.bfloat16)
    upto = jnp.where(square_row <= square_column, 1.0, 0.0).astype(jnp.bfloat16)
    within = jnp.dot(flags, upto, preferred_element_type=F32)
    rows = jnp.broadcast_to(within[:, LANES - 1 :], (16, LANES)).astype(jnp.bfloat16)
    below = jnp.where(square_column[0:16, 0:16] < square_row[0:16, 0:16], 1.0, 0.0).astype(jnp.bfloat16)
    before = jnp.dot(below, rows, preferred_element_type=F32)
    rank = jnp.where(active, (within + before).astype(I32) - 1, -1)
    rank_ref[...] = rank
    number = jnp.sum(jnp.where(active, 1, 0))
    number_ref[0] = number
    row8 = lax.broadcasted_iota(I32, (8, LANES), 0)
    column8 = lax.broadcasted_iota(I32, (8, LANES), 1)

    def compact(turn, carry):
        sums = jnp.zeros((8, LANES), F32)
        for r in range(16):
            hit = jnp.where(rank[r : r + 1] - turn * LANES == square_row, 1.0, 0.0).astype(jnp.bfloat16)
            mine = mark[r : r + 1]
            facts = jnp.where(row8 == 0, mine >> 7, jnp.where(row8 == 1, mine & 127, jnp.where(row8 == 2, r, column8)))
            sums = sums + lax.dot_general(
                facts.astype(F32).astype(jnp.bfloat16), hit, contract, preferred_element_type=F32
            )
        mark_of = (sums[0:1] * 128.0 + sums[1:2]).astype(I32)
        block, lane = split_position(mark_of - 1, sizes)
        block_ref[pl.ds(turn, 1), :] = jnp.where(mark_of > 0, block, -1)
        lane_ref[pl.ds(turn, 1), :] = jnp.where(mark_of > 0, lane, 0)
        star_row = jnp.broadcast_to(sums[2:3], (8, LANES)).astype(I32)
        star_lane = jnp.broadcast_to(sums[3:4], (8, LANES)).astype(I32)
        head = jnp.zeros((8, LANES), F32)
        tail = jnp.zeros((8, LANES), F32)
        for r in range(16):
            part = slice(r * LANES, (r + 1) * LANES)
            here = star_row == r
            head = jnp.where(here, take(state_ref[0:8, part], star_lane), head)
            rest = jnp.concatenate(
                [state_ref[8:12, part], jnp.broadcast_to(elapsed_ref[:, part], (4, LANES))], axis=0
            )
            tail = jnp.where(here, take(rest, star_lane), tail)
        pos, vel = head[0:3], head[3:6]
        accel = jnp.concatenate([head[6:8], tail[0:1]], axis=0)
        jerk = tail[1:4]
        step_time = tail[4:5]
        half = step_time * 0.5
        twelfth = step_time * step_time / 12.0
        known_vel = vel + accel * half + jerk * twelfth
        known_pos = pos + (vel + known_vel) * half + accel * twelfth
        none = jnp.zeros((2, LANES), F32)
        wide3 = lambda value: jnp.broadcast_to(value, (3, LANES))
        begin = pl.ds(pl.multiple_of(turn * 8, 8), 8)
        known_ref[begin, :] = jnp.concatenate([known_pos, known_vel, none], axis=0)
        one_ref[begin, :] = jnp.concatenate([wide3(half * half - twelfth), wide3(half), none], axis=0)
        two_ref[begin, :] = jnp.concatenate([wide3(twelfth * half), wide3(twelfth), none], axis=0)
        return carry

    lax.fori_loop(0, jnp.maximum(((number + 255) >> 8) * 2, 2), compact, 0)


def pair_kernel(
    counts_ref, own_ref, one_ref, two_ref, three_ref, mine_ref, other_ref, out_ref,
    splat_ref, source_ref, part_ref, sum_ref,
):
    _, live = list_offsets(counts_ref)
    size = jnp.where(lax.axis_index("c") == 0, *two_sizes(live))
    column = lax.broadcasted_iota(I32, (8, LANES), 1)
    zero = jnp.zeros((8, LANES), F32)
    halves = (mine_ref, other_ref)
    targets = own_ref[...] + one_ref[...] + two_ref[...] + three_ref[...]

    for v in range(SETS):
        for c in range(7):
            at = (c * SETS + v) * 8
            source_ref[at : at + 8, :] = halves[v >> 3][pl.ds((v & 7) * 64 + c, 8, stride=8), :]

    def one_half(half):
        mine = targets[half * 8 : half * 8 + 8]
        count = jnp.minimum(size - half * LANES, LANES)

        def splat(chunk):
            for t in range(chunk * 32, chunk * 32 + 32):
                values = take(mine, jnp.full((8, LANES), t, I32))
                for c in range(6):
                    at = (t * 6 + c) * 8
                    splat_ref[at : at + 8, :] = jnp.broadcast_to(values[c : c + 1], (8, LANES))

        splat(0)
        for chunk in range(1, 4):
            pl.when(count > chunk * 32)(functools.partial(splat, chunk))

        def four_targets(turn, carry):
            first = turn * 4
            sums = [zero] * 36
            for v in range(SETS):
                sx, sy, sz, vx, vy, vz, mass = [
                    source_ref[(c * SETS + v) * 8 : (c * SETS + v) * 8 + 8, :] for c in range(7)
                ]
                for t in range(4):
                    tx, ty, tz, ux, uy, uz = [
                        splat_ref[pl.ds(pl.multiple_of(((first + t) * 6 + c) * 8, 8), 8), :]
                        for c in range(6)
                    ]
                    rx = sx - tx
                    ry = sy - ty
                    rz = sz - tz
                    wx = vx - ux
                    wy = vy - uy
                    wz = vz - uz
                    square = (rx * rx + softening_square) + ry * ry + rz * rz
                    dot = rx * wx + ry * wy + rz * wz
                    inverse = lax.rsqrt(square)
                    inverse2 = inverse * inverse
                    weight = (mass * inverse) * inverse2
                    radial = dot * inverse2
                    pulls = (weight * rx, weight * ry, weight * rz)
                    drifts = (weight * wx, weight * wy, weight * wz)
                    for c in range(3):
                        sums[t * 9 + c] = sums[t * 9 + c] + pulls[c]
                        sums[t * 9 + 3 + c] = sums[t * 9 + 3 + c] + drifts[c]
                        sums[t * 9 + 6 + c] = sums[t * 9 + 6 + c] + radial * pulls[c]
            for t in range(4):
                for c in range(6):
                    total = sums[t * 9 + c]
                    if c >= 3:
                        total = total - 3.0 * sums[t * 9 + 3 + c]
                    part_ref[pl.ds(pl.multiple_of((c * LANES + first + t) * 8, 8), 8), :] = total
            return carry

        lax.fori_loop(0, (count + 3) >> 2, four_targets, 0)

        def gather_sums(octets):
            for o in octets:
                one_octet(o)

        def one_octet(o):
            row = zero
            for c in range(6):
                first = (c * LANES + o * 8) * 8
                total = part_ref[pl.ds(first, 8, stride=8), :]
                for k in range(1, 8):
                    total = total + part_ref[pl.ds(first + k, 8, stride=8), :]
                row = jnp.where(column == c, jnp.sum(total, axis=1, keepdims=True), row)
            sum_ref[o * 8 : o * 8 + 8, :] = row

        gather_sums(range(4))
        for chunk in range(1, 4):
            pl.when(count > chunk * 32)(functools.partial(gather_sums, range(chunk * 4, chunk * 4 + 4)))
        out_ref[half * 8 : half * 8 + 8, :] = sum_ref[...].T[0:8]

    one_half(0)

    @pl.when(size <= LANES)
    def _():
        out_ref[8:16, :] = zero

    @pl.when(size > LANES)
    def _():
        one_half(1)


def combine_kernel(own_ref, one_ref, two_ref, three_ref, out_ref, rest_ref):
    force = own_ref[...] + one_ref[...] + two_ref[...] + three_ref[...]
    for peer in range(32):
        out_ref[peer] = force[0:8]
    rest_ref[...] = force[8:16]


def finish_kernel(
    half, number_ref, first_ref, rank_ref, block_ref, lane_ref, slot_block_ref, slot_lane_ref, known_ref, one_ref, two_ref,
    mine_ref, other_ref, state_ref, *refs,
):
    new_ref, active_ref = refs[-2:]
    core = lax.axis_index("c")
    zero = jnp.zeros((8, LANES), F32)

    def wide(row):
        return jnp.broadcast_to(row, (8, LANES))

    def group_of(block):
        return jnp.where((block & 1) == half, block >> 1, -1)

    wanted = [group_of(wide(slot_block_ref[b : b + 1, :])) for b in range(CAP // LANES)]
    lanes = [wide(slot_lane_ref[b : b + 1, :]) for b in range(CAP // LANES)]
    firsts = [first_ref[b] for b in range(CAP // LANES)]

    def span(turn, acc):
        acc = list(acc)
        for b in range(CAP // LANES):
            group = jnp.minimum(firsts[b] + turn, GROUPS - 1)
            rows = pl.ds(pl.multiple_of((group & 31) * 8, 8), 8)
            forces = jnp.where((group >> 5) == core, mine_ref[rows, :], other_ref[rows, :])
            acc[b] = jnp.where(wanted[b] == group, take(forces, lanes[b]), acc[b])
        return tuple(acc)

    found = (zero,) * (CAP // LANES)
    for turn in range(3):
        found = span(jnp.int32(turn), found)
    found = lax.fori_loop(3, first_ref[CAP // LANES], span, found)
    for b in range(CAP // LANES):
        part = slice(b * LANES, (b + 1) * LANES)
        if half == 0:
            active_ref[:, part] = found[b][0:6]
        else:
            active_ref[:, part] = jnp.where(wanted[b][0:6] >= 0, found[b][0:6], refs[0][:, part])

    new_ref[...] = state_ref[...]
    none = jnp.zeros((2, LANES), F32)

    def moved(turn):
        group = group_of(wide(block_ref[pl.ds(turn, 1), :]))
        lane = wide(lane_ref[pl.ds(turn, 1), :])
        seen = group ^ (core * 32)
        force = zero
        for g in range(GROUPS):
            half_ref = mine_ref if g < 32 else other_ref
            force = jnp.where(seen == g, take(half_ref[(g & 31) * 8 : (g & 31) * 8 + 8, :], lane), force)
        begin = pl.ds(pl.multiple_of(turn * 8, 8), 8)
        accel = jnp.concatenate([force[0:3], force[0:3], none], axis=0)
        jerk = jnp.concatenate([force[3:6], force[3:6], none], axis=0)
        place = known_ref[begin, :] + accel * one_ref[begin, :] - jerk * two_ref[begin, :]
        head = jnp.concatenate([place[0:6], force[0:2]], axis=0)
        flag = jnp.where(group[0:4] >= 0, 1.0, 0.0)
        return head, jnp.concatenate([force[2:6], flag], axis=0)

    def compact(turn, carry):
        tiles = [moved(turn * 2), moved(turn * 2 + 1)]
        for r in range(16):
            part = slice(r * LANES, (r + 1) * LANES)
            rank = wide(rank_ref[r : r + 1, :])
            place = rank & 127
            top, bottom = new_ref[0:8, part], new_ref[8:12, part]
            for k, (head, tail) in enumerate(tiles):
                got = take(tail, place)
                here = (rank >> 7) == turn * 2 + k
                if half == 1:
                    here = here & (wide(got[7:8]) > 0.5)
                top = jnp.where(here, take(head, place), top)
                bottom = jnp.where(here[0:4], got[0:4], bottom)
            new_ref[0:8, part] = top
            new_ref[8:12, part] = bottom
        return carry

    compact(jnp.int32(0), 0)
    lax.fori_loop(1, (number_ref[0] + 255) >> 8, compact, 0)


def exchange_y(part):
    return [lax.ppermute(part, "y", [(i, (i + k) % 4) for i in range(4)]) for k in range(1, 4)]


def in_vmem(*arrays):
    return [pltpu.with_memory_space_constraint(array, pltpu.VMEM) for array in arrays]


def spread(part, *done):
    part = lax.all_to_all(part, ("z", "x"), 0, 0).reshape(-1, LANES)
    part, *done = lax.optimization_barrier((part, *done))
    return in_vmem(part, lax.ppermute(part, "c", [(0, 1), (1, 0)])), done


def finish(half, plan, forces, state, *rest):
    return pl.pallas_call(
        functools.partial(finish_kernel, half),
        out_shape=[
            jax.ShapeDtypeStruct((12, SHARD), F32),
            jax.ShapeDtypeStruct((6, CAP), F32),
        ],
        in_specs=[SMEM] * 2 + [VMEM] * (11 + len(rest)),
        out_specs=[VMEM, VMEM],
        name="finish",
    )(*plan[:2], *in_vmem(*plan[2:]), *forces, *in_vmem(state, *rest))


def body(state, mass, elapsed, active_ids, active_count):
    mass = mass.reshape(1, SHARD)
    elapsed = elapsed.reshape(1, SHARD)
    ids = active_ids.reshape(1, CAP)
    packed = pl.pallas_call(
        pack_kernel,
        out_shape=pltpu.VMEM((32, 16, LANES), F32),
        in_specs=[VMEM] * 4,
        out_specs=VMEM,
        name="pack",
    )(state, mass, elapsed, ids)
    slab, _ = spread(packed)
    own = pl.pallas_call(
        extract_kernel,
        out_shape=pltpu.VMEM((16, LANES), F32),
        in_specs=[SMEM, VMEM, VMEM],
        out_specs=VMEM,
        name="extract",
    )(active_count, *slab)
    others = exchange_y(own)
    square = pltpu.VMEM((LANES, LANES), F32)
    plan = pl.pallas_call(
        plan_kernel,
        out_shape=[jax.ShapeDtypeStruct((1,), I32), jax.ShapeDtypeStruct((CAP // LANES + 1,), I32)]
        + [pltpu.VMEM((16, LANES), I32)] * 5
        + [square] * 3,
        in_specs=[SMEM] + [VMEM] * 4,
        out_specs=[SMEM] * 2 + [VMEM] * 8,
        name="plan",
    )(active_count, *slab, *in_vmem(state, elapsed))
    partial = pl.pallas_call(
        pair_kernel,
        out_shape=pltpu.VMEM((16, LANES), F32),
        in_specs=[SMEM] + [VMEM] * 6,
        out_specs=VMEM,
        scratch_shapes=[
            pltpu.VMEM((LANES * 6 * 8, LANES), F32),
            pltpu.VMEM((7 * SETS * 8, LANES), F32),
            pltpu.VMEM((6 * LANES * 8, LANES), F32),
            pltpu.VMEM((LANES, LANES), F32),
        ],
        compiler_params=pltpu.CompilerParams(vmem_limit_bytes=24 * 2**20),
        name="pairs",
    )(active_count, *in_vmem(own, *others), *slab)
    combined, rest = pl.pallas_call(
        combine_kernel,
        out_shape=[pltpu.VMEM((32, 8, LANES), F32), pltpu.VMEM((8, LANES), F32)],
        in_specs=[VMEM] * 4,
        out_specs=[VMEM] * 2,
        name="combine",
    )(*in_vmem(partial, *exchange_y(partial)))
    turns = (group_size(jnp.sum(active_count)) > LANES).astype(I32)
    forces, (turns, *plan) = spread(combined, turns, *plan)
    outputs = finish(0, plan, forces, state)

    def more(carry):
        turn, new_state, active_force = carry
        forces, _ = spread(jnp.broadcast_to(rest[None], (32, 8, LANES)))
        return (turn + 1, *finish(1, plan, forces, new_state, active_force))

    return lax.while_loop(lambda carry: carry[0] < turns, more, (jnp.int32(0), *outputs))[1:]


def solution(mesh):
    fine = Mesh(mesh.devices.reshape(4, 2, 4, 8), ("x", "c", "y", "z"))
    placed = (P(None, ("y", "z")), P(("y", "z")), P(("y", "z")), P(("x", "c")), P())
    return jax.shard_map(
        body,
        mesh=fine,
        in_specs=placed,
        out_specs=(P(None, ("y", "z")), P(None, ("x", "c"))),
        check_vma=False,
    )
```
